32 devices in a mesh: box: 8 (over y, x, core), dir: 4 (over z).
Axes of the slice: x: 2, y: 2, z: 4, core: 2. Of those that a mesh axis runs over, the one named last changes fastest.
Arguments:
- children: bfloat16 [8, 8, 128, 4, 512], P('box', None, 'dir'), may hold values from -6 to 6
- legendre: bfloat16 [512, 256, 128], P('dir'), may hold values from -0.5 to 0.5
- axial_angle: float32 [2, 256], replicated, may hold values from -3.140625 to 3.140625
- planar_angle: float32 [4, 256, 512], P(None, 'dir'), may hold values from -3.140625 to 3.140625
- translator: bfloat16 [32, 2, 256, 512], P(None, None, 'dir'), may hold values from -0.8984375 to 0.8984375
- group_slot: int32 [8], P('box'), may hold values from 0 to 7, as said below
- source_list: int32 [8, 8], P('box'), may hold values from 0 to 7, as said below
- offset_list: int32 [8, 8], P('box'), may hold values from 0 to 31
- row_counts: int32 [8], P('box'), may hold values from 1 to 8
Outputs:
- incoming: bfloat16 [8, 256, 4, 512], P('box', 'dir')
The draws below stay inside these ranges and needn't reach their ends.
Inputs may be any that keep to these rules, and one draw needn't show every extreme that they name: `group_slot`: each block of 1 row, one index of box, holds a permutation of that block's own row numbers. `source_list`: names a box group of the destination's own block of 1 row or of the block just before or just after it, never the destination itself.
All inputs are finite; a program needn't handle non-finite values.
Results may differ from the reference program's by a relative error of at most 0.0057.
Values may be sent and summed in bfloat16 or wider, within the bound.
A program may use at most 128 MiB of HBM per device.

```python
import jax
import jax.numpy as jnp
from jax import lax

NTC = 128
NTH = 256
NPH = 512
NOFF = 32
MAXL = 8
GRP_DEV = 1
GROUPS = 8


def draw_group_slot(key, part):
    blocks = GROUPS // GRP_DEV
    subkeys = jax.random.split(key, blocks)
    orders = jax.vmap(lambda subkey: jax.random.permutation(subkey, GRP_DEV))(subkeys)
    shifted = orders + jnp.arange(blocks)[:, None] * GRP_DEV
    return shifted.reshape(GROUPS).astype(jnp.int32)


def draw_source_list(key, part):
    blocks = GROUPS // GRP_DEV
    destination = jnp.arange(GROUPS)
    device = destination // GRP_DEV
    lower = jnp.maximum(device - 1, 0) * GRP_DEV
    upper = jnp.minimum(device + 2, blocks) * GRP_DEV
    spread = upper - lower - 1
    raw_draw = jax.random.randint(key, (GROUPS, MAXL), 0, 1 << 20)
    candidate = lower[:, None] + raw_draw % spread[:, None]
    result = jnp.where(candidate >= destination[:, None], candidate + 1, candidate)
    return result.astype(jnp.int32)


def draw_row_counts(key, part):
    raw_draw = jax.random.randint(key, (GROUPS,), 1, MAXL + 1)
    chosen = jax.random.randint(jax.random.fold_in(key, 7), (), 0, GROUPS)
    result = jnp.where(jnp.arange(GROUPS) == chosen, MAXL, raw_draw)
    return result.astype(jnp.int32)


def plant(array, key, least, top_value):
    longest = array.shape.index(max(array.shape))
    spots = []
    for shift in (0, 1):
        where = [jax.random.randint(jax.random.fold_in(key, axis), (), 0, length) for axis, length in enumerate(array.shape)]
        where[longest] = (where[longest] + shift) % array.shape[longest]
        spots.append(tuple(where))
    return array.at[spots[0]].set(least).at[spots[1]].set(top_value)


def shard_levels(own_key, shape, pieces, low, top_value):
    def one(dim, parts):
        draws = jax.random.uniform(jax.random.fold_in(jax.random.fold_in(own_key, 6), dim), (parts,), jnp.float32, low / len(pieces), top_value / len(pieces))
        return jnp.repeat(jnp.exp(draws), shape[dim] // parts).reshape((-1,) + (1,) * (len(shape) - dim - 1))

    level = one(*pieces[0])
    for cut in pieces[1:]:
        level = level * one(*cut)
    return level


def normal_values(rng, shape, width, most, cuts=(), held_as=jnp.bfloat16):
    drawn = jax.random.normal(rng, shape, jnp.float32) * width
    if len(cuts) > 0:
        drawn = shard_levels(rng, shape, cuts, -0.22, 0.18) * drawn
    return jnp.clip(drawn, min=-most, max=most).astype(held_as)


def setup_inputs(seed: int = 0) -> dict:
    splits = jax.random.split(jax.random.key(seed), 10)
    return {
        "children": normal_values(splits[0], (GROUPS, 8, NTC, 4, NPH), 1.0, 6.0, ((0, 8), (2, 4))),
        "legendre": normal_values(splits[1], (NPH, NTH, NTC), NTC ** -0.5, 0.5, ((0, 4),)),
        "axial_angle": jnp.clip(jax.random.uniform(splits[2], (2, NTH), jnp.float32, -3.140625, 3.140625), -3.140625, 3.140625),
        "planar_angle": jnp.clip(jax.random.uniform(splits[3], (4, NTH, NPH), jnp.float32, -3.140625, 3.140625), -3.140625, 3.140625),
        "translator": normal_values(splits[4], (NOFF, 2, NTH, NPH), 0.15, 0.8984375, ((2, 4),)),
        "group_slot": draw_group_slot(jax.random.fold_in(splits[9], 71), 0),
        "source_list": draw_source_list(jax.random.fold_in(splits[9], 71), 0),
        "offset_list": plant(jax.random.randint(splits[7], (GROUPS, MAXL), 0, NOFF), jax.random.fold_in(splits[7], 1), 0, NOFF - 1).astype(jnp.int32),
        "row_counts": draw_row_counts(jax.random.fold_in(splits[9], 71), 0),
    }


def aggregate(child, legendre, axial_angle, planar_angle):
    values = child.astype(jnp.float32).reshape(8, NTC, 2, 2, NPH)
    samples = values[:, :, :, 0, :] + 1j * values[:, :, :, 1, :]
    spectrum = jnp.fft.fft(samples, axis=-1, norm="ortho")
    modes_real = jnp.real(spectrum).astype(jnp.bfloat16).astype(jnp.float32)
    modes_imag = jnp.imag(spectrum).astype(jnp.bfloat16).astype(jnp.float32)
    matrices = legendre.astype(jnp.float32)
    interp_real = jnp.einsum("mtq,kqpm->ktpm", matrices, modes_real).reshape(2, 4, NTH, 2, NPH)
    interp_imag = jnp.einsum("mtq,kqpm->ktpm", matrices, modes_imag).reshape(2, 4, NTH, 2, NPH)
    axial_cos = jnp.cos(axial_angle)[:, None, :, None, None]
    axial_sin = jnp.sin(axial_angle)[:, None, :, None, None]
    pairs_real = jnp.sum(interp_real * axial_cos - interp_imag * axial_sin, axis=0)
    pairs_imag = jnp.sum(interp_real * axial_sin + interp_imag * axial_cos, axis=0)
    field = jnp.fft.ifft(pairs_real + 1j * pairs_imag, axis=-1, norm="ortho")
    field_real = jnp.real(field)
    field_imag = jnp.imag(field)
    planar_cos = jnp.cos(planar_angle)[:, :, None, :]
    planar_sin = jnp.sin(planar_angle)[:, :, None, :]
    stored_real = jnp.sum(field_real * planar_cos - field_imag * planar_sin, axis=0)
    stored_imag = jnp.sum(field_real * planar_sin + field_imag * planar_cos, axis=0)
    stored = jnp.stack([stored_real, stored_imag], axis=2)
    return stored.reshape(NTH, 4, NPH).astype(jnp.bfloat16)


def reference(children, legendre, axial_angle, planar_angle, translator, group_slot, source_list, offset_list, row_counts):
    stored = lax.map(lambda child: aggregate(child, legendre, axial_angle, planar_angle), children)
    inverse = jnp.argsort(group_slot).astype(jnp.int32)
    parent = stored[inverse]
    total_real = jnp.zeros((GROUPS, NTH, 2, NPH), jnp.float32)
    total_imag = jnp.zeros((GROUPS, NTH, 2, NPH), jnp.float32)
    for slot in range(MAXL):
        picked = parent[source_list[:, slot]].astype(jnp.float32).reshape(GROUPS, NTH, 2, 2, NPH)
        operator = translator[offset_list[:, slot]].astype(jnp.float32)
        live = (slot < row_counts).astype(jnp.float32)[:, None, None, None]
        oper_real = operator[:, 0, :, None, :] * live
        oper_imag = operator[:, 1, :, None, :] * live
        total_real = total_real + oper_real * picked[:, :, :, 0, :] - oper_imag * picked[:, :, :, 1, :]
        total_imag = total_imag + oper_real * picked[:, :, :, 1, :] + oper_imag * picked[:, :, :, 0, :]
    result = jnp.stack([total_real, total_imag], axis=3).reshape(GROUPS, NTH, 4, NPH)
    return result.astype(jnp.bfloat16)
```

```python
import functools
import math

import jax
import jax.numpy as jnp
import ml_dtypes
import numpy as np
from jax import lax
from jax.experimental import pallas as pl
from jax.experimental.pallas import tpu as pltpu
from jax.sharding import PartitionSpec as P

MESH = pl.DeviceIdType.MESH
F32 = jnp.float32
BF16 = jnp.bfloat16
LANES = 128


def extended(x, sides, width):
    for axis, dim in sides:
        peers, length = (lax.axis_size(axis), x.shape[dim])
        up = [(i, (i + 1) % peers) for i in range(peers - 1)]
        down = [(j, i) for i, j in up]
        last = lax.slice_in_dim(x, length - width, length, axis=dim)
        initial = lax.slice_in_dim(x, 0, width, axis=dim)
        before = lax.ppermute(last, axis, up)
        after = lax.ppermute(initial, axis, down)
        x = jnp.concatenate([before, x, after], axis=dim)
    return x


def dft_tables(length):
    samples = jnp.arange(length, dtype=jnp.int32)
    product = samples[:, None] * samples[None, :] % length
    phase = product.astype(jnp.float32) * (2.0 * math.pi / length)
    cosine = jnp.cos(phase) / math.sqrt(length)
    sine = jnp.sin(phase) / math.sqrt(length)
    return (cosine, sine)


def general(
    children,
    legendre,
    axial_angle,
    planar_angle,
    translator,
    group_slot,
    source_list,
    offset_list,
    row_counts,
):
    local_groups, kids, rows_in, comps, length = children.shape
    dir_count = lax.axis_size("dir")
    box_index = lax.axis_index("box")
    modes_local = legendre.shape[0]
    rows_out = legendre.shape[1] // dir_count
    cosine, sine = dft_tables(length)
    high = lax.Precision.HIGH
    values = children.astype(jnp.float32).reshape(local_groups, kids, rows_in, 2, 2, length)
    samples_real = values[..., 0, :]
    samples_imag = values[..., 1, :]
    spec_real = jnp.einsum("gkqpj,jm->mgkpq", samples_real, cosine, precision=high) + jnp.einsum(
        "gkqpj,jm->mgkpq", samples_imag, sine, precision=high
    )
    spec_imag = jnp.einsum("gkqpj,jm->mgkpq", samples_imag, cosine, precision=high) - jnp.einsum(
        "gkqpj,jm->mgkpq", samples_real, sine, precision=high
    )
    spectrum = jnp.stack([spec_real, spec_imag], axis=4)
    spectrum = spectrum.astype(jnp.bfloat16).reshape(
        1, length, local_groups * kids * comps * rows_in
    )
    received = lax.all_to_all(spectrum, "dir", split_axis=1, concat_axis=0, tiled=True)
    received = received.reshape(dir_count, modes_local, local_groups * kids * comps, rows_in)
    matrices = legendre.reshape(modes_local, dir_count, rows_out, dir_count, rows_in)
    interp = jnp.einsum("mabsq,smcq->macb", matrices, received, preferred_element_type=jnp.float32)
    interp = interp.reshape(modes_local, dir_count, local_groups, 2, 4, 2, 2, rows_out)
    angles = jnp.transpose(axial_angle.reshape(2, dir_count, rows_out), (1, 0, 2))
    axial_cos = jnp.cos(angles)[None, :, None, :, None, None, :]
    axial_sin = jnp.sin(angles)[None, :, None, :, None, None, :]
    part_real = interp[..., 0, :]
    part_imag = interp[..., 1, :]
    pairs_real = jnp.sum(part_real * axial_cos - part_imag * axial_sin, axis=3)
    pairs_imag = jnp.sum(part_real * axial_sin + part_imag * axial_cos, axis=3)
    pairs = jnp.stack([pairs_real, pairs_imag], axis=5)
    pairs = pairs.reshape(modes_local, dir_count, local_groups * 4 * 2 * 2 * rows_out)
    returned = lax.all_to_all(pairs, "dir", split_axis=1, concat_axis=0, tiled=True)
    combined = returned.reshape(length, local_groups, 4, 2, 2, rows_out)
    comb_real = combined[:, :, :, :, 0, :]
    comb_imag = combined[:, :, :, :, 1, :]
    field_real = jnp.einsum("mgxpb,mj->gxbpj", comb_real, cosine, precision=high) - jnp.einsum(
        "mgxpb,mj->gxbpj", comb_imag, sine, precision=high
    )
    field_imag = jnp.einsum("mgxpb,mj->gxbpj", comb_real, sine, precision=high) + jnp.einsum(
        "mgxpb,mj->gxbpj", comb_imag, cosine, precision=high
    )
    planar_cos = jnp.cos(planar_angle)[None, :, :, None, :]
    planar_sin = jnp.sin(planar_angle)[None, :, :, None, :]
    stored_real = jnp.sum(field_real * planar_cos - field_imag * planar_sin, axis=1)
    stored_imag = jnp.sum(field_real * planar_sin + field_imag * planar_cos, axis=1)
    stored = jnp.stack([stored_real, stored_imag], axis=3)
    stored = stored.reshape(local_groups, rows_out, comps, length).astype(jnp.bfloat16)
    local_slot = group_slot - box_index * local_groups
    placement = (local_slot[None, :] == jnp.arange(local_groups)[:, None]).astype(jnp.bfloat16)
    ordered = jnp.einsum("lk,kbcj->lbcj", placement, stored, preferred_element_type=jnp.float32)
    ordered = ordered.astype(jnp.bfloat16)
    window = extended(ordered, (("box", 0),), local_groups)
    relative = source_list - (box_index - 1) * local_groups
    near = (relative[..., None] == jnp.arange(window.shape[0])).astype(jnp.bfloat16)
    picked = jnp.einsum("glw,wbcj->glbcj", near, window, preferred_element_type=jnp.float32)
    picked = picked.reshape(local_groups, source_list.shape[1], rows_out, 2, 2, length)
    chosen = (offset_list[..., None] == jnp.arange(translator.shape[0])).astype(jnp.bfloat16)
    operator = jnp.einsum("glo,orbj->glrbj", chosen, translator, preferred_element_type=jnp.float32)
    live = (jnp.arange(source_list.shape[1])[None, :] < row_counts[:, None]).astype(jnp.float32)
    live = live[:, :, None, None, None]
    oper_real = operator[:, :, 0, :, None, :].astype(jnp.float32) * live
    oper_imag = operator[:, :, 1, :, None, :].astype(jnp.float32) * live
    picked_real = picked[..., 0, :].astype(jnp.float32)
    picked_imag = picked[..., 1, :].astype(jnp.float32)
    total_real = jnp.sum(oper_real * picked_real - oper_imag * picked_imag, axis=1)
    total_imag = jnp.sum(oper_real * picked_imag + oper_imag * picked_real, axis=1)
    result = jnp.stack([total_real, total_imag], axis=3).reshape(
        local_groups, rows_out, comps, length
    )
    return result.astype(jnp.bfloat16)


PARTS = 2
CHUNKS = 2 * PARTS


def forward_table(length, dirs):
    phase = np.outer(np.arange(length), np.arange(length)) % length * (2.0 * np.pi / length)
    cosine, sine = np.cos(phase), np.sin(phase)
    both = np.stack(
        [np.concatenate([cosine, sine], axis=1), np.concatenate([-sine, cosine], axis=1)], axis=0
    )
    both = both.reshape(2, dirs, PARTS, length // dirs // PARTS, 2 * length)
    both = both.transpose(2, 1, 0, 3, 4).reshape(PARTS, -1, 2 * length)
    return both.astype(ml_dtypes.bfloat16)


def inverse_table(length):
    phase = np.outer(np.arange(length), np.arange(length)) % length * (2.0 * np.pi / length)
    cosine, sine = np.cos(phase) / length, np.sin(phase) / length
    both = np.concatenate(
        [np.concatenate([cosine, sine], axis=1), np.concatenate([-sine, cosine], axis=1)], axis=0
    )
    return both.astype(ml_dtypes.bfloat16)


def fused(
    dirs,
    boxes,
    source_hbm,
    offset_hbm,
    count_hbm,
    x_hbm,
    wf_hbm,
    axial_hbm,
    legendre_hbm,
    wi_hbm,
    planar_hbm,
    translator_hbm,
    out_ref,
    source_ref,
    offset_ref,
    count_ref,
    x_ref,
    wf_ref,
    axial_ref,
    legendre_ref,
    wi_ref,
    planar_ref,
    translator_ref,
    samples,
    send1,
    recv1,
    spread,
    pairs,
    send2,
    recv2,
    planar_cos,
    planar_sin,
    sums,
    stored,
    halo,
    local_sems,
    index_sems,
    send1_sems,
    recv1_sems,
    send2_sems,
    recv2_sems,
    halo_send,
    halo_recv,
):
    me = lax.axis_index("dir")
    box = lax.axis_index("box")
    right, left = lax.rem(box + 1, boxes), lax.rem(box + boxes - 1, boxes)
    rows_out, length = planar_ref.shape[1:]
    own = legendre_ref.shape[0]
    modes = own // PARTS
    rows_in = LANES // dirs
    slots = source_ref.shape[1]
    peers = (me + 1 - 2 * lax.rem(me, 2), lax.rem(me + 2, 4), 3 - me)
    order = (1, 2, 0)

    barrier = pltpu.get_barrier_semaphore()
    for peer in peers:
        pl.semaphore_signal(barrier, inc=1, device_id=(box, peer), device_id_type=MESH)
    for peer in (left, right):
        pl.semaphore_signal(barrier, inc=1, device_id=(peer, me), device_id_type=MESH)

    def load(src, dst, sem):
        return pltpu.make_async_copy(src, dst, sem)

    load_x = load(x_hbm, x_ref, local_sems.at[0])
    load_wf = [load(wf_hbm.at[i], wf_ref.at[i], local_sems.at[1 + i]) for i in range(PARTS)]
    at = 1 + PARTS
    load_planar = load(planar_hbm, planar_ref, local_sems.at[at])
    load_translator = load(translator_hbm, translator_ref, local_sems.at[at + 1])
    load_legendre = load(legendre_hbm, legendre_ref, local_sems.at[at + 2])
    load_axial = load(axial_hbm, axial_ref, local_sems.at[at + 3])
    load_wi = load(wi_hbm, wi_ref, local_sems.at[at + 4])
    load_index = [
        load(src, dst, index_sems.at[i])
        for i, (src, dst) in enumerate(
            ((source_hbm, source_ref), (offset_hbm, offset_ref), (count_hbm, count_ref))
        )
    ]
    for item in (load_x, *load_wf):
        item.start()

    def out_copy(chunk, step):
        return pltpu.make_async_remote_copy(
            src_ref=send1.at[chunk, peers[step]],
            dst_ref=recv1.at[chunk, me],
            send_sem=send1_sems.at[chunk, step],
            recv_sem=recv1_sems.at[chunk, step],
            device_id=(box, peers[step]),
            device_id_type=MESH,
        )

    place = pl.ds(pl.multiple_of(me * own, own), own)

    def back_copy(p, h, step):
        return pltpu.make_async_remote_copy(
            src_ref=send2.at[p, h, peers[step]],
            dst_ref=recv2.at[p, h, :, place, :],
            send_sem=send2_sems.at[p, h, step],
            recv_sem=recv2_sems.at[p, h, step],
            device_id=(box, peers[step]),
            device_id_type=MESH,
        )

    comps = LANES // rows_in
    to = lax.broadcasted_iota(jnp.int32, (LANES, LANES), 0)
    come = lax.broadcasted_iota(jnp.int32, (LANES, LANES), 1)
    sorting = ((to % rows_in) * comps + to // rows_in == come).astype(F32).astype(BF16)
    load_x.wait()
    for k in range(x_ref.shape[0]):
        sorted_rows = jnp.dot(
            sorting, x_ref[k].reshape(LANES, length), preferred_element_type=F32
        ).astype(BF16)
        for c in range(comps):
            p, r = c // 2, c % 2
            row = (p * x_ref.shape[0] + k) * rows_in
            samples[row : row + rows_in, r * length : (r + 1) * length] = sorted_rows[
                c * rows_in : (c + 1) * rows_in
            ]
    cols = samples.shape[0] // 2

    for chunk in range(CHUNKS):
        p, part = chunk // PARTS, chunk % PARTS
        if p == 0:
            load_wf[part].wait()
        spectrum = lax.dot_general(
            wf_ref[part],
            samples[p * cols : (p + 1) * cols],
            (((1,), (1,)), ((), ())),
            preferred_element_type=F32,
        )
        send1[chunk] = spectrum.astype(BF16).reshape(send1.shape[1:])
        if chunk == 0:
            pl.semaphore_wait(barrier, dirs + 1)
        out_copy(chunk, 1).start()
        out_copy(chunk, 2).start()
        if chunk == 0:
            for item in (load_planar, *load_index, load_translator, load_axial, load_legendre, load_wi):
                item.start()
        if part == PARTS - 1:
            for i in range(PARTS):
                out_copy(p * PARTS + i, 0).start()
        recv1[chunk, me] = send1[chunk, me]

    load_planar.wait()
    for q in range(4):
        planar_cos[q] = jnp.cos(planar_ref[q])
        planar_sin[q] = jnp.sin(planar_ref[q])
    for item in load_index:
        item.wait()
    load_translator.wait()
    sums[...] = jnp.zeros_like(sums)

    def gather(slot, carry):
        source, op = source_ref[0, slot], offset_ref[0, slot]
        live = slot < count_ref[0]
        before = jnp.where(jnp.logical_and(live, source < box), 1.0, 0.0)
        after = jnp.where(jnp.logical_and(live, source > box), 1.0, 0.0)
        for r in range(2):
            tile = translator_ref[op, r].astype(F32)
            sums[0, r] += before * tile
            sums[1, r] += after * tile
        return carry

    lax.fori_loop(0, slots, gather, 0)

    load_axial.wait()
    kids = x_ref.shape[0]
    theta = axial_ref.shape[1]
    upper = lax.broadcasted_iota(jnp.int32, (kids, theta), 0) < kids // 2
    angle = jnp.where(upper, axial_ref[0:1], axial_ref[1:2])
    axial_cos, axial_sin = jnp.cos(angle), jnp.sin(angle)
    block = lax.broadcasted_iota(jnp.int32, (modes, LANES), 1) // rows_in
    load_legendre.wait()

    def exchanged(tiles, a):
        out = tiles[a]
        for s in range(4):
            if s != a:
                shift = ((s - a) * rows_in) % LANES
                out = jnp.where(block == s, pltpu.roll(tiles[s], shift, 1), out)
        return out

    def interpolate(p, part):
        chunk = p * PARTS + part
        for step in range(3):
            out_copy(chunk, step).wait_recv()
        for r in range(2):
            for g in range(kids // dirs):
                tiles = [
                    recv1[
                        chunk, s, r * modes : (r + 1) * modes, g * LANES : (g + 1) * LANES
                    ].astype(F32)
                    for s in range(dirs)
                ]
                for a in range(dirs):
                    spread[pl.ds(r * kids + g * dirs + a, modes, stride=2 * kids), :] = exchanged(
                        tiles, a
                    )
        first = part * modes

        def mode(i, inner):
            rows = spread[pl.ds(pl.multiple_of(i * 2 * kids, 2 * kids), 2 * kids), :]
            value = lax.dot_general(
                rows.astype(BF16),
                legendre_ref[first + i],
                (((1,), (1,)), ((), ())),
                preferred_element_type=F32,
            )
            real, imag = value[:kids], value[kids:]
            sum_real = real * axial_cos - imag * axial_sin
            sum_imag = real * axial_sin + imag * axial_cos
            both = jnp.where(
                upper,
                sum_real + pltpu.roll(sum_real, kids // 2, 0),
                sum_imag + pltpu.roll(sum_imag, kids // 2, 0),
            )
            for n in range(pairs.shape[0]):
                tile = pairs.at[n]
                tile[pl.ds(i, kids, stride=modes), :] = both[:, n * LANES : (n + 1) * LANES]
            return inner

        lax.fori_loop(0, modes, mode, 0, unroll=8)
        rows = pl.ds(pl.multiple_of(first, modes), modes)
        for n in range(pairs.shape[0]):
            for r in range(2):
                tiles = [
                    pairs[n, (r * 4 + q) * modes : (r * 4 + q + 1) * modes, :] for q in range(4)
                ]
                for g in range(4):
                    send2[p, g % 2, 2 * n + g // 2, r, rows] = exchanged(tiles, g).astype(BF16)

    for p in range(2):

        def both_parts(part, carry, p=p):
            interpolate(p, part)
            return carry

        lax.fori_loop(0, PARTS, both_parts, 0)
        for h, step in ((0, 1), (1, 1), (0, 2), (1, 2), (0, 0), (1, 0)):
            back_copy(p, h, step).start()
        for h in range(2):
            recv2[p, h, :, place, :] = send2[p, h, me]

    load_wi.wait()
    has = (box < boxes - 1, box > 0)

    def move(p, h, side):
        return pltpu.make_async_remote_copy(
            src_ref=stored.at[p, h],
            dst_ref=halo.at[side, p, h],
            send_sem=halo_send.at[side, p, h],
            recv_sem=halo_recv.at[side, p, h],
            device_id=((right, left)[side], me),
            device_id_type=MESH,
        )

    rows_half = rows_out // 2
    pieces = [(p, h) for p in range(2) for h in range(2)]
    for p, h in pieces:
        for step in range(3):
            back_copy(p, h, step).wait_recv()
        field = lax.dot_general(
            recv2[p, h].reshape(-1, LANES),
            wi_ref[...],
            (((0,), (0,)), ((), ())),
            preferred_element_type=F32,
        )
        total_real, total_imag = 0.0, 0.0
        for q in range(4):
            cos = planar_cos[q, h * rows_half : (h + 1) * rows_half]
            sin = planar_sin[q, h * rows_half : (h + 1) * rows_half]
            real = field[q * rows_half : (q + 1) * rows_half, :length]
            imag = field[q * rows_half : (q + 1) * rows_half, length:]
            total_real = total_real + (real * cos - imag * sin)
            total_imag = total_imag + (real * sin + imag * cos)
        stored[p, h, 0] = total_real.astype(BF16)
        stored[p, h, 1] = total_imag.astype(BF16)
        for side in range(2):
            pl.when(has[side])(move(p, h, side).start)
    for step in range(3):
        for chunk in range(CHUNKS):
            out_copy(chunk, step).wait_send()
        for p, h in pieces:
            back_copy(p, h, step).wait_send()
    for p, h in pieces:
        for side in range(2):
            pl.when(has[side])(move(p, h, side).wait_send)
            pl.when(has[1 - side])(move(p, h, side).wait_recv)
        real, imag = 0.0, 0.0
        mine = slice(h * rows_half, (h + 1) * rows_half)
        for side in range(2):
            source_real = jnp.where(has[1 - side], halo[side, p, h, 0].astype(F32), 0.0)
            source_imag = jnp.where(has[1 - side], halo[side, p, h, 1].astype(F32), 0.0)
            weight_real, weight_imag = sums[side, 0, mine], sums[side, 1, mine]
            real = real + (weight_real * source_real - weight_imag * source_imag)
            imag = imag + (weight_real * source_imag + weight_imag * source_real)
        out_ref[2 * p, mine] = real.astype(BF16)
        out_ref[2 * p + 1, mine] = imag.astype(BF16)


def shards(
    children,
    legendre,
    axial_angle,
    planar_angle,
    translator,
    group_slot,
    source_list,
    offset_list,
    row_counts,
):
    local_groups, kids, rows_in, comps, length = children.shape
    dirs = lax.axis_size("dir")
    boxes = lax.axis_size("box")
    modes_local, theta_out, theta_in = legendre.shape
    rows_out = theta_out // dirs
    fits = (
        local_groups == 1
        and dirs == 4
        and boxes > 2
        and kids == 8
        and comps == 4
        and theta_in == LANES
        and 2 * rows_out == LANES
        and modes_local == LANES
    )
    if not fits:
        return general(
            children,
            legendre,
            axial_angle,
            planar_angle,
            translator,
            group_slot,
            source_list,
            offset_list,
            row_counts,
        )
    rows = kids * 2 * rows_in
    forward = jnp.asarray(forward_table(length, dirs))
    modes = modes_local // PARTS
    vmem = pl.BlockSpec(memory_space=pltpu.VMEM)
    hbm = pl.BlockSpec(memory_space=pltpu.HBM)
    inverse = jnp.asarray(inverse_table(length))
    exchange = pltpu.SemaphoreType.DMA((CHUNKS, dirs - 1))
    back = pltpu.SemaphoreType.DMA((2, 2, dirs - 1))
    out = pl.pallas_call(
        functools.partial(fused, dirs, boxes),
        out_shape=jax.ShapeDtypeStruct((comps, rows_out, length), BF16),
        in_specs=[hbm] * 10,
        out_specs=vmem,
        scratch_shapes=[
            pltpu.SMEM(source_list.shape, jnp.int32),
            pltpu.SMEM(offset_list.shape, jnp.int32),
            pltpu.SMEM(row_counts.shape, jnp.int32),
            pltpu.VMEM(children.shape[1:], BF16),
            pltpu.VMEM(forward.shape, BF16),
            pltpu.VMEM(axial_angle.shape, F32),
            pltpu.VMEM(legendre.shape, BF16),
            pltpu.VMEM(inverse.shape, BF16),
            pltpu.VMEM(planar_angle.shape, F32),
            pltpu.VMEM(translator.shape, BF16),
            pltpu.VMEM((rows, 2 * length), BF16),
            pltpu.VMEM((CHUNKS, dirs, 2 * modes, rows // 2), BF16),
            pltpu.VMEM((CHUNKS, dirs, 2 * modes, rows // 2), BF16),
            pltpu.VMEM((modes * kids * 2, LANES), F32),
            pltpu.VMEM((theta_out // LANES, 8 * modes, LANES), F32),
            pltpu.VMEM((2, 2, dirs, 2, modes_local, LANES), BF16),
            pltpu.VMEM((2, 2, 2, length, LANES), BF16),
            pltpu.VMEM(planar_angle.shape, F32),
            pltpu.VMEM(planar_angle.shape, F32),
            pltpu.VMEM((2, 2, rows_out, length), F32),
            pltpu.VMEM((2, 2, 2, rows_out // 2, length), BF16),
            pltpu.VMEM((2, 2, 2, 2, rows_out // 2, length), BF16),
            pltpu.SemaphoreType.DMA((6 + PARTS,)),
            pltpu.SemaphoreType.DMA((3,)),
            exchange,
            exchange,
            back,
            back,
            pltpu.SemaphoreType.DMA((2, 2, 2)),
            pltpu.SemaphoreType.DMA((2, 2, 2)),
        ],
        compiler_params=pltpu.CompilerParams(
            collective_id=0, has_side_effects=True, vmem_limit_bytes=60 * 1024 * 1024
        ),
    )(
        source_list,
        offset_list,
        row_counts,
        children[0],
        forward,
        axial_angle,
        legendre,
        inverse,
        planar_angle,
        translator,
    )
    return out.transpose(1, 0, 2)[None]


def solution(mesh):
    placed = (
        P("box", None, "dir", None, None),
        P("dir", None, None),
        P(),
        P(None, "dir", None),
        P(None, None, "dir", None),
        P("box"),
        P("box", None),
        P("box", None),
        P("box"),
    )
    return jax.shard_map(
        shards, mesh=mesh, in_specs=placed, out_specs=P("box", "dir", None, None), check_vma=False
    )
```

```python
import functools
import math

import jax
import jax.numpy as jnp
import ml_dtypes
import numpy as np
from jax import lax
from jax.experimental import pallas as pl
from jax.experimental.pallas import tpu as pltpu
from jax.sharding import PartitionSpec as P

MESH = pl.DeviceIdType.MESH
F32 = jnp.float32
BF16 = jnp.bfloat16
LANES = 128


def extended(x, sides, width):
    for axis, dim in sides:
        peers, length = (lax.axis_size(axis), x.shape[dim])
        up = [(i, (i + 1) % peers) for i in range(peers - 1)]
        down = [(j, i) for i, j in up]
        last = lax.slice_in_dim(x, length - width, length, axis=dim)
        initial = lax.slice_in_dim(x, 0, width, axis=dim)
        before = lax.ppermute(last, axis, up)
        after = lax.ppermute(initial, axis, down)
        x = jnp.concatenate([before, x, after], axis=dim)
    return x


def dft_tables(length):
    samples = jnp.arange(length, dtype=jnp.int32)
    product = samples[:, None] * samples[None, :] % length
    phase = product.astype(jnp.float32) * (2.0 * math.pi / length)
    cosine = jnp.cos(phase) / math.sqrt(length)
    sine = jnp.sin(phase) / math.sqrt(length)
    return (cosine, sine)


def general(
    children,
    legendre,
    axial_angle,
    planar_angle,
    translator,
    group_slot,
    source_list,
    offset_list,
    row_counts,
):
    local_groups, kids, rows_in, comps, length = children.shape
    dir_count = lax.axis_size("dir")
    box_index = lax.axis_index("box")
    modes_local = legendre.shape[0]
    rows_out = legendre.shape[1] // dir_count
    cosine, sine = dft_tables(length)
    high = lax.Precision.HIGH
    values = children.astype(jnp.float32).reshape(local_groups, kids, rows_in, 2, 2, length)
    samples_real = values[..., 0, :]
    samples_imag = values[..., 1, :]
    spec_real = jnp.einsum("gkqpj,jm->mgkpq", samples_real, cosine, precision=high) + jnp.einsum(
        "gkqpj,jm->mgkpq", samples_imag, sine, precision=high
    )
    spec_imag = jnp.einsum("gkqpj,jm->mgkpq", samples_imag, cosine, precision=high) - jnp.einsum(
        "gkqpj,jm->mgkpq", samples_real, sine, precision=high
    )
    spectrum = jnp.stack([spec_real, spec_imag], axis=4)
    spectrum = spectrum.astype(jnp.bfloat16).reshape(
        1, length, local_groups * kids * comps * rows_in
    )
    received = lax.all_to_all(spectrum, "dir", split_axis=1, concat_axis=0, tiled=True)
    received = received.reshape(dir_count, modes_local, local_groups * kids * comps, rows_in)
    matrices = legendre.reshape(modes_local, dir_count, rows_out, dir_count, rows_in)
    interp = jnp.einsum("mabsq,smcq->macb", matrices, received, preferred_element_type=jnp.float32)
    interp = interp.reshape(modes_local, dir_count, local_groups, 2, 4, 2, 2, rows_out)
    angles = jnp.transpose(axial_angle.reshape(2, dir_count, rows_out), (1, 0, 2))
    axial_cos = jnp.cos(angles)[None, :, None, :, None, None, :]
    axial_sin = jnp.sin(angles)[None, :, None, :, None, None, :]
    part_real = interp[..., 0, :]
    part_imag = interp[..., 1, :]
    pairs_real = jnp.sum(part_real * axial_cos - part_imag * axial_sin, axis=3)
    pairs_imag = jnp.sum(part_real * axial_sin + part_imag * axial_cos, axis=3)
    pairs = jnp.stack([pairs_real, pairs_imag], axis=5)
    pairs = pairs.reshape(modes_local, dir_count, local_groups * 4 * 2 * 2 * rows_out)
    returned = lax.all_to_all(pairs, "dir", split_axis=1, concat_axis=0, tiled=True)
    combined = returned.reshape(length, local_groups, 4, 2, 2, rows_out)
    comb_real = combined[:, :, :, :, 0, :]
    comb_imag = combined[:, :, :, :, 1, :]
    field_real = jnp.einsum("mgxpb,mj->gxbpj", comb_real, cosine, precision=high) - jnp.einsum(
        "mgxpb,mj->gxbpj", comb_imag, sine, precision=high
    )
    field_imag = jnp.einsum("mgxpb,mj->gxbpj", comb_real, sine, precision=high) + jnp.einsum(
        "mgxpb,mj->gxbpj", comb_imag, cosine, precision=high
    )
    planar_cos = jnp.cos(planar_angle)[None, :, :, None, :]
    planar_sin = jnp.sin(planar_angle)[None, :, :, None, :]
    stored_real = jnp.sum(field_real * planar_cos - field_imag * planar_sin, axis=1)
    stored_imag = jnp.sum(field_real * planar_sin + field_imag * planar_cos, axis=1)
    stored = jnp.stack([stored_real, stored_imag], axis=3)
    stored = stored.reshape(local_groups, rows_out, comps, length).astype(jnp.bfloat16)
    local_slot = group_slot - box_index * local_groups
    placement = (local_slot[None, :] == jnp.arange(local_groups)[:, None]).astype(jnp.bfloat16)
    ordered = jnp.einsum("lk,kbcj->lbcj", placement, stored, preferred_element_type=jnp.float32)
    ordered = ordered.astype(jnp.bfloat16)
    window = extended(ordered, (("box", 0),), local_groups)
    relative = source_list - (box_index - 1) * local_groups
    near = (relative[..., None] == jnp.arange(window.shape[0])).astype(jnp.bfloat16)
    picked = jnp.einsum("glw,wbcj->glbcj", near, window, preferred_element_type=jnp.float32)
    picked = picked.reshape(local_groups, source_list.shape[1], rows_out, 2, 2, length)
    chosen = (offset_list[..., None] == jnp.arange(translator.shape[0])).astype(jnp.bfloat16)
    operator = jnp.einsum("glo,orbj->glrbj", chosen, translator, preferred_element_type=jnp.float32)
    live = (jnp.arange(source_list.shape[1])[None, :] < row_counts[:, None]).astype(jnp.float32)
    live = live[:, :, None, None, None]
    oper_real = operator[:, :, 0, :, None, :].astype(jnp.float32) * live
    oper_imag = operator[:, :, 1, :, None, :].astype(jnp.float32) * live
    picked_real = picked[..., 0, :].astype(jnp.float32)
    picked_imag = picked[..., 1, :].astype(jnp.float32)
    total_real = jnp.sum(oper_real * picked_real - oper_imag * picked_imag, axis=1)
    total_imag = jnp.sum(oper_real * picked_imag + oper_imag * picked_real, axis=1)
    result = jnp.stack([total_real, total_imag], axis=3).reshape(
        local_groups, rows_out, comps, length
    )
    return result.astype(jnp.bfloat16)


PARTS = 2
CHUNKS = 2 * PARTS


def forward_table(length, dirs):
    phase = np.outer(np.arange(length), np.arange(length)) % length * (2.0 * np.pi / length)
    cosine, sine = np.cos(phase), np.sin(phase)
    both = np.stack(
        [np.concatenate([cosine, sine], axis=1), np.concatenate([-sine, cosine], axis=1)], axis=0
    )
    both = both.reshape(2, dirs, PARTS, length // dirs // PARTS, 2 * length)
    both = both.transpose(2, 1, 0, 3, 4).reshape(PARTS, -1, 2 * length)
    return both.astype(ml_dtypes.bfloat16)


def inverse_table(length):
    phase = np.outer(np.arange(length), np.arange(length)) % length * (2.0 * np.pi / length)
    cosine, sine = np.cos(phase) / length, np.sin(phase) / length
    both = np.concatenate(
        [np.concatenate([cosine, sine], axis=1), np.concatenate([-sine, cosine], axis=1)], axis=0
    )
    return both.astype(ml_dtypes.bfloat16)


def fused(
    dirs,
    boxes,
    source_hbm,
    offset_hbm,
    count_hbm,
    x_hbm,
    wf_hbm,
    axial_hbm,
    legendre_hbm,
    wi_hbm,
    planar_hbm,
    translator_hbm,
    out_ref,
    source_ref,
    offset_ref,
    count_ref,
    x_ref,
    wf_ref,
    axial_ref,
    legendre_ref,
    wi_ref,
    planar_ref,
    translator_ref,
    samples,
    send1,
    recv1,
    spread,
    pairs,
    send2,
    recv2,
    planar_cos,
    planar_sin,
    sums,
    stored,
    halo,
    local_sems,
    index_sems,
    send1_sems,
    recv1_sems,
    send2_sems,
    recv2_sems,
    halo_send,
    halo_recv,
):
    me = lax.axis_index("dir")
    box = lax.axis_index("box")
    right, left = lax.rem(box + 1, boxes), lax.rem(box + boxes - 1, boxes)
    rows_out, length = planar_ref.shape[1:]
    own = legendre_ref.shape[0]
    modes = own // PARTS
    rows_in = LANES // dirs
    slots = source_ref.shape[1]
    peers = (me + 1 - 2 * lax.rem(me, 2), lax.rem(me + 2, 4), 3 - me)
    order = (1, 2, 0)

    barrier = pltpu.get_barrier_semaphore()
    for peer in peers:
        pl.semaphore_signal(barrier, inc=1, device_id=(box, peer), device_id_type=MESH)
    for peer in (left, right):
        pl.semaphore_signal(barrier, inc=1, device_id=(peer, me), device_id_type=MESH)

    def load(src, dst, sem):
        return pltpu.make_async_copy(src, dst, sem)

    load_x = load(x_hbm, x_ref, local_sems.at[0])
    load_wf = [load(wf_hbm.at[i], wf_ref.at[i], local_sems.at[1 + i]) for i in range(PARTS)]
    at = 1 + PARTS
    load_planar = load(planar_hbm, planar_ref, local_sems.at[at])
    load_translator = load(translator_hbm, translator_ref, local_sems.at[at + 1])
    load_legendre = load(legendre_hbm, legendre_ref, local_sems.at[at + 2])
    load_axial = load(axial_hbm, axial_ref, local_sems.at[at + 3])
    load_wi = load(wi_hbm, wi_ref, local_sems.at[at + 4])
    load_index = [
        load(src, dst, index_sems.at[i])
        for i, (src, dst) in enumerate(
            ((source_hbm, source_ref), (offset_hbm, offset_ref), (count_hbm, count_ref))
        )
    ]
    for item in (load_x, *load_wf):
        item.start()

    def out_copy(chunk, step):
        return pltpu.make_async_remote_copy(
            src_ref=send1.at[chunk, peers[step]],
            dst_ref=recv1.at[chunk, me],
            send_sem=send1_sems.at[chunk, step],
            recv_sem=recv1_sems.at[chunk, step],
            device_id=(box, peers[step]),
            device_id_type=MESH,
        )

    place = pl.ds(pl.multiple_of(me * own, own), own)

    def back_copy(p, h, step):
        return pltpu.make_async_remote_copy(
            src_ref=send2.at[p, h, peers[step]],
            dst_ref=recv2.at[p, h, :, place, :],
            send_sem=send2_sems.at[p, h, step],
            recv_sem=recv2_sems.at[p, h, step],
            device_id=(box, peers[step]),
            device_id_type=MESH,
        )

    comps = LANES // rows_in
    to = lax.broadcasted_iota(jnp.int32, (LANES, LANES), 0)
    come = lax.broadcasted_iota(jnp.int32, (LANES, LANES), 1)
    sorting = ((to % rows_in) * comps + to // rows_in == come).astype(F32).astype(BF16)
    load_x.wait()
    for k in range(x_ref.shape[0]):
        sorted_rows = jnp.dot(
            sorting, x_ref[k].reshape(LANES, length), preferred_element_type=F32
        ).astype(BF16)
        for c in range(comps):
            p, r = c // 2, c % 2
            row = (p * x_ref.shape[0] + k) * rows_in
            samples[row : row + rows_in, r * length : (r + 1) * length] = sorted_rows[
                c * rows_in : (c + 1) * rows_in
            ]
    cols = samples.shape[0] // 2

    for chunk in range(CHUNKS):
        p, part = chunk // PARTS, chunk % PARTS
        if p == 0:
            load_wf[part].wait()
        spectrum = lax.dot_general(
            wf_ref[part],
            samples[p * cols : (p + 1) * cols],
            (((1,), (1,)), ((), ())),
            preferred_element_type=F32,
        )
        send1[chunk] = spectrum.astype(BF16).reshape(send1.shape[1:])
        if chunk == 0:
            pl.semaphore_wait(barrier, dirs + 1)
        out_copy(chunk, 1).start()
        out_copy(chunk, 2).start()
        if chunk == 0:
            for item in (load_planar, *load_index, load_translator, load_axial, load_legendre, load_wi):
                item.start()
        if part == PARTS - 1:
            for i in range(PARTS):
                out_copy(p * PARTS + i, 0).start()
        recv1[chunk, me] = send1[chunk, me]

    load_planar.wait()
    for q in range(4):
        planar_cos[q] = jnp.cos(planar_ref[q])
        planar_sin[q] = jnp.sin(planar_ref[q])
    for item in load_index:
        item.wait()
    load_translator.wait()
    sums[...] = jnp.zeros_like(sums)

    def gather(slot, carry):
        source, op = source_ref[0, slot], offset_ref[0, slot]
        live = slot < count_ref[0]
        before = jnp.where(jnp.logical_and(live, source < box), 1.0, 0.0)
        after = jnp.where(jnp.logical_and(live, source > box), 1.0, 0.0)
        for r in range(2):
            tile = translator_ref[op, r].astype(F32)
            sums[0, r] += before * tile
            sums[1, r] += after * tile
        return carry

    lax.fori_loop(0, slots, gather, 0)

    load_axial.wait()
    kids = x_ref.shape[0]
    theta = axial_ref.shape[1]
    upper = lax.broadcasted_iota(jnp.int32, (kids, theta), 0) < kids // 2
    angle = jnp.where(upper, axial_ref[0:1], axial_ref[1:2])
    axial_cos, axial_sin = jnp.cos(angle), jnp.sin(angle)
    block = lax.broadcasted_iota(jnp.int32, (modes, LANES), 1) // rows_in
    load_legendre.wait()

    def exchanged(tiles, a):
        out = tiles[a]
        for s in range(4):
            if s != a:
                shift = ((s - a) * rows_in) % LANES
                out = jnp.where(block == s, pltpu.roll(tiles[s], shift, 1), out)
        return out

    def interpolate(p, part):
        chunk = p * PARTS + part
        for step in range(3):
            out_copy(chunk, step).wait_recv()
        for r in range(2):
            for g in range(kids // dirs):
                tiles = [
                    recv1[
                        chunk, s, r * modes : (r + 1) * modes, g * LANES : (g + 1) * LANES
                    ].astype(F32)
                    for s in range(dirs)
                ]
                for a in range(dirs):
                    spread[pl.ds(r * kids + g * dirs + a, modes, stride=2 * kids), :] = exchanged(
                        tiles, a
                    )
        first = part * modes

        def mode(i, inner):
            rows = spread[pl.ds(pl.multiple_of(i * 2 * kids, 2 * kids), 2 * kids), :]
            value = lax.dot_general(
                rows.astype(BF16),
                legendre_ref[first + i],
                (((1,), (1,)), ((), ())),
                preferred_element_type=F32,
            )
            real, imag = value[:kids], value[kids:]
            sum_real = real * axial_cos - imag * axial_sin
            sum_imag = real * axial_sin + imag * axial_cos
            both = jnp.where(
                upper,
                sum_real + pltpu.roll(sum_real, kids // 2, 0),
                sum_imag + pltpu.roll(sum_imag, kids // 2, 0),
            )
            for n in range(pairs.shape[0]):
                tile = pairs.at[n]
                tile[pl.ds(i, kids, stride=modes), :] = both[:, n * LANES : (n + 1) * LANES]
            return inner

        lax.fori_loop(0, modes, mode, 0, unroll=8)
        rows = pl.ds(pl.multiple_of(first, modes), modes)
        for n in range(pairs.shape[0]):
            for r in range(2):
                tiles = [
                    pairs[n, (r * 4 + q) * modes : (r * 4 + q + 1) * modes, :] for q in range(4)
                ]
                for g in range(4):
                    send2[p, g % 2, 2 * n + g // 2, r, rows] = exchanged(tiles, g).astype(BF16)

    for p in range(2):

        def both_parts(part, carry, p=p):
            interpolate(p, part)
            return carry

        lax.fori_loop(0, PARTS, both_parts, 0)
        for h, step in ((0, 1), (1, 1), (0, 2), (1, 2), (0, 0), (1, 0)):
            back_copy(p, h, step).start()
        for h in range(2):
            recv2[p, h, :, place, :] = send2[p, h, me]

    load_wi.wait()
    has = (box < boxes - 1, box > 0)

    def move(p, h, side):
        return pltpu.make_async_remote_copy(
            src_ref=stored.at[p, h],
            dst_ref=halo.at[side, p, h],
            send_sem=halo_send.at[side, p, h],
            recv_sem=halo_recv.at[side, p, h],
            device_id=((right, left)[side], me),
            device_id_type=MESH,
        )

    rows_half = rows_out // 2
    pieces = [(p, h) for p in range(2) for h in range(2)]
    for p, h in pieces:
        for step in range(3):
            back_copy(p, h, step).wait_recv()
        field = lax.dot_general(
            recv2[p, h].reshape(-1, LANES),
            wi_ref[...],
            (((0,), (0,)), ((), ())),
            preferred_element_type=F32,
        )
        total_real, total_imag = 0.0, 0.0
        for q in range(4):
            cos = planar_cos[q, h * rows_half : (h + 1) * rows_half]
            sin = planar_sin[q, h * rows_half : (h + 1) * rows_half]
            real = field[q * rows_half : (q + 1) * rows_half, :length]
            imag = field[q * rows_half : (q + 1) * rows_half, length:]
            total_real = total_real + (real * cos - imag * sin)
            total_imag = total_imag + (real * sin + imag * cos)
        stored[p, h, 0] = total_real.astype(BF16)
        stored[p, h, 1] = total_imag.astype(BF16)
        for side in range(2):
            pl.when(has[side])(move(p, h, side).start)
    for step in range(3):
        for chunk in range(CHUNKS):
            out_copy(chunk, step).wait_send()
        for p, h in pieces:
            back_copy(p, h, step).wait_send()
    for p, h in pieces:
        for side in range(2):
            pl.when(has[side])(move(p, h, side).wait_send)
            pl.when(has[1 - side])(move(p, h, side).wait_recv)
        real, imag = 0.0, 0.0
        mine = slice(h * rows_half, (h + 1) * rows_half)
        for side in range(2):
            source_real = jnp.where(has[1 - side], halo[side, p, h, 0].astype(F32), 0.0)
            source_imag = jnp.where(has[1 - side], halo[side, p, h, 1].astype(F32), 0.0)
            weight_real, weight_imag = sums[side, 0, mine], sums[side, 1, mine]
            real = real + (weight_real * source_real - weight_imag * source_imag)
            imag = imag + (weight_real * source_imag + weight_imag * source_real)
        out_ref[2 * p, mine] = real.astype(BF16)
        out_ref[2 * p + 1, mine] = imag.astype(BF16)


def shards(
    children,
    legendre,
    axial_angle,
    planar_angle,
    translator,
    group_slot,
    source_list,
    offset_list,
    row_counts,
):
    local_groups, kids, rows_in, comps, length = children.shape
    dirs = lax.axis_size("dir")
    boxes = lax.axis_size("box")
    modes_local, theta_out, theta_in = legendre.shape
    rows_out = theta_out // dirs
    fits = (
        local_groups == 1
        and dirs == 4
        and boxes > 2
        and kids == 8
        and comps == 4
        and theta_in == LANES
        and 2 * rows_out == LANES
        and modes_local == LANES
    )
    if not fits:
        return general(
            children,
            legendre,
            axial_angle,
            planar_angle,
            translator,
            group_slot,
            source_list,
            offset_list,
            row_counts,
        )
    rows = kids * 2 * rows_in
    forward = jnp.asarray(forward_table(length, dirs))
    modes = modes_local // PARTS
    vmem = pl.BlockSpec(memory_space=pltpu.VMEM)
    hbm = pl.BlockSpec(memory_space=pltpu.HBM)
    inverse = jnp.asarray(inverse_table(length))
    exchange = pltpu.SemaphoreType.DMA((CHUNKS, dirs - 1))
    back = pltpu.SemaphoreType.DMA((2, 2, dirs - 1))
    out = pl.pallas_call(
        functools.partial(fused, dirs, boxes),
        out_shape=jax.ShapeDtypeStruct((comps, rows_out, length), BF16),
        in_specs=[hbm] * 10,
        out_specs=vmem,
        scratch_shapes=[
            pltpu.SMEM(source_list.shape, jnp.int32),
            pltpu.SMEM(offset_list.shape, jnp.int32),
            pltpu.SMEM(row_counts.shape, jnp.int32),
            pltpu.VMEM(children.shape[1:], BF16),
            pltpu.VMEM(forward.shape, BF16),
            pltpu.VMEM(axial_angle.shape, F32),
            pltpu.VMEM(legendre.shape, BF16),
            pltpu.VMEM(inverse.shape, BF16),
            pltpu.VMEM(planar_angle.shape, F32),
            pltpu.VMEM(translator.shape, BF16),
            pltpu.VMEM((rows, 2 * length), BF16),
            pltpu.VMEM((CHUNKS, dirs, 2 * modes, rows // 2), BF16),
            pltpu.VMEM((CHUNKS, dirs, 2 * modes, rows // 2), BF16),
            pltpu.VMEM((modes * kids * 2, LANES), F32),
            pltpu.VMEM((theta_out // LANES, 8 * modes, LANES), F32),
            pltpu.VMEM((2, 2, dirs, 2, modes_local, LANES), BF16),
            pltpu.VMEM((2, 2, 2, length, LANES), BF16),
            pltpu.VMEM(planar_angle.shape, F32),
            pltpu.VMEM(planar_angle.shape, F32),
            pltpu.VMEM((2, 2, rows_out, length), F32),
            pltpu.VMEM((2, 2, 2, rows_out // 2, length), BF16),
            pltpu.VMEM((2, 2, 2, 2, rows_out // 2, length), BF16),
            pltpu.SemaphoreType.DMA((6 + PARTS,)),
            pltpu.SemaphoreType.DMA((3,)),
            exchange,
            exchange,
            back,
            back,
            pltpu.SemaphoreType.DMA((2, 2, 2)),
            pltpu.SemaphoreType.DMA((2, 2, 2)),
        ],
        compiler_params=pltpu.CompilerParams(
            collective_id=0, has_side_effects=True, vmem_limit_bytes=40 * 1024 * 1024
        ),
    )(
        pltpu.with_memory_space_constraint(source_list, pltpu.HBM),
        pltpu.with_memory_space_constraint(offset_list, pltpu.HBM),
        row_counts,
        *(
            pltpu.with_memory_space_constraint(item, pltpu.HBM)
            for item in (
                children[0],
                forward,
                axial_angle,
                legendre,
                inverse,
                planar_angle,
                translator,
            )
        ),
    )
    return out.transpose(1, 0, 2)[None]


def solution(mesh):
    placed = (
        P("box", None, "dir", None, None),
        P("dir", None, None),
        P(),
        P(None, "dir", None),
        P(None, None, "dir", None),
        P("box"),
        P("box", None),
        P("box", None),
        P("box"),
    )
    return jax.shard_map(
        shards, mesh=mesh, in_specs=placed, out_specs=P("box", "dir", None, None), check_vma=False
    )
```

```python
import functools
import math

import jax
import jax.numpy as jnp
import ml_dtypes
import numpy as np
from jax import lax
from jax.experimental import pallas as pl
from jax.experimental.pallas import tpu as pltpu
from jax.sharding import PartitionSpec as P

MESH = pl.DeviceIdType.MESH
F32 = jnp.float32
BF16 = jnp.bfloat16
LANES = 128


def extended(x, sides, width):
    for axis, dim in sides:
        peers, length = (lax.axis_size(axis), x.shape[dim])
        up = [(i, (i + 1) % peers) for i in range(peers - 1)]
        down = [(j, i) for i, j in up]
        last = lax.slice_in_dim(x, length - width, length, axis=dim)
        initial = lax.slice_in_dim(x, 0, width, axis=dim)
        before = lax.ppermute(last, axis, up)
        after = lax.ppermute(initial, axis, down)
        x = jnp.concatenate([before, x, after], axis=dim)
    return x


def dft_tables(length):
    samples = jnp.arange(length, dtype=jnp.int32)
    product = samples[:, None] * samples[None, :] % length
    phase = product.astype(jnp.float32) * (2.0 * math.pi / length)
    cosine = jnp.cos(phase) / math.sqrt(length)
    sine = jnp.sin(phase) / math.sqrt(length)
    return (cosine, sine)


def general(
    children,
    legendre,
    axial_angle,
    planar_angle,
    translator,
    group_slot,
    source_list,
    offset_list,
    row_counts,
):
    local_groups, kids, rows_in, comps, length = children.shape
    dir_count = lax.axis_size("dir")
    box_index = lax.axis_index("box")
    modes_local = legendre.shape[0]
    rows_out = legendre.shape[1] // dir_count
    cosine, sine = dft_tables(length)
    high = lax.Precision.HIGH
    values = children.astype(jnp.float32).reshape(local_groups, kids, rows_in, 2, 2, length)
    samples_real = values[..., 0, :]
    samples_imag = values[..., 1, :]
    spec_real = jnp.einsum("gkqpj,jm->mgkpq", samples_real, cosine, precision=high) + jnp.einsum(
        "gkqpj,jm->mgkpq", samples_imag, sine, precision=high
    )
    spec_imag = jnp.einsum("gkqpj,jm->mgkpq", samples_imag, cosine, precision=high) - jnp.einsum(
        "gkqpj,jm->mgkpq", samples_real, sine, precision=high
    )
    spectrum = jnp.stack([spec_real, spec_imag], axis=4)
    spectrum = spectrum.astype(jnp.bfloat16).reshape(
        1, length, local_groups * kids * comps * rows_in
    )
    received = lax.all_to_all(spectrum, "dir", split_axis=1, concat_axis=0, tiled=True)
    received = received.reshape(dir_count, modes_local, local_groups * kids * comps, rows_in)
    matrices = legendre.reshape(modes_local, dir_count, rows_out, dir_count, rows_in)
    interp = jnp.einsum("mabsq,smcq->macb", matrices, received, preferred_element_type=jnp.float32)
    interp = interp.reshape(modes_local, dir_count, local_groups, 2, 4, 2, 2, rows_out)
    angles = jnp.transpose(axial_angle.reshape(2, dir_count, rows_out), (1, 0, 2))
    axial_cos = jnp.cos(angles)[None, :, None, :, None, None, :]
    axial_sin = jnp.sin(angles)[None, :, None, :, None, None, :]
    part_real = interp[..., 0, :]
    part_imag = interp[..., 1, :]
    pairs_real = jnp.sum(part_real * axial_cos - part_imag * axial_sin, axis=3)
    pairs_imag = jnp.sum(part_real * axial_sin + part_imag * axial_cos, axis=3)
    pairs = jnp.stack([pairs_real, pairs_imag], axis=5)
    pairs = pairs.reshape(modes_local, dir_count, local_groups * 4 * 2 * 2 * rows_out)
    returned = lax.all_to_all(pairs, "dir", split_axis=1, concat_axis=0, tiled=True)
    combined = returned.reshape(length, local_groups, 4, 2, 2, rows_out)
    comb_real = combined[:, :, :, :, 0, :]
    comb_imag = combined[:, :, :, :, 1, :]
    field_real = jnp.einsum("mgxpb,mj->gxbpj", comb_real, cosine, precision=high) - jnp.einsum(
        "mgxpb,mj->gxbpj", comb_imag, sine, precision=high
    )
    field_imag = jnp.einsum("mgxpb,mj->gxbpj", comb_real, sine, precision=high) + jnp.einsum(
        "mgxpb,mj->gxbpj", comb_imag, cosine, precision=high
    )
    planar_cos = jnp.cos(planar_angle)[None, :, :, None, :]
    planar_sin = jnp.sin(planar_angle)[None, :, :, None, :]
    stored_real = jnp.sum(field_real * planar_cos - field_imag * planar_sin, axis=1)
    stored_imag = jnp.sum(field_real * planar_sin + field_imag * planar_cos, axis=1)
    stored = jnp.stack([stored_real, stored_imag], axis=3)
    stored = stored.reshape(local_groups, rows_out, comps, length).astype(jnp.bfloat16)
    local_slot = group_slot - box_index * local_groups
    placement = (local_slot[None, :] == jnp.arange(local_groups)[:, None]).astype(jnp.bfloat16)
    ordered = jnp.einsum("lk,kbcj->lbcj", placement, stored, preferred_element_type=jnp.float32)
    ordered = ordered.astype(jnp.bfloat16)
    window = extended(ordered, (("box", 0),), local_groups)
    relative = source_list - (box_index - 1) * local_groups
    near = (relative[..., None] == jnp.arange(window.shape[0])).astype(jnp.bfloat16)
    picked = jnp.einsum("glw,wbcj->glbcj", near, window, preferred_element_type=jnp.float32)
    picked = picked.reshape(local_groups, source_list.shape[1], rows_out, 2, 2, length)
    chosen = (offset_list[..., None] == jnp.arange(translator.shape[0])).astype(jnp.bfloat16)
    operator = jnp.einsum("glo,orbj->glrbj", chosen, translator, preferred_element_type=jnp.float32)
    live = (jnp.arange(source_list.shape[1])[None, :] < row_counts[:, None]).astype(jnp.float32)
    live = live[:, :, None, None, None]
    oper_real = operator[:, :, 0, :, None, :].astype(jnp.float32) * live
    oper_imag = operator[:, :, 1, :, None, :].astype(jnp.float32) * live
    picked_real = picked[..., 0, :].astype(jnp.float32)
    picked_imag = picked[..., 1, :].astype(jnp.float32)
    total_real = jnp.sum(oper_real * picked_real - oper_imag * picked_imag, axis=1)
    total_imag = jnp.sum(oper_real * picked_imag + oper_imag * picked_real, axis=1)
    result = jnp.stack([total_real, total_imag], axis=3).reshape(
        local_groups, rows_out, comps, length
    )
    return result.astype(jnp.bfloat16)


PARTS = 2
CHUNKS = 2 * PARTS
PIECES = 4
EXCHANGE = 32


def forward_table(length, dirs):
    phase = np.outer(np.arange(length), np.arange(length)) % length * (2.0 * np.pi / length)
    cosine, sine = np.cos(phase), np.sin(phase)
    both = np.stack(
        [np.concatenate([cosine, sine], axis=1), np.concatenate([-sine, cosine], axis=1)], axis=0
    )
    both = both.reshape(2, dirs, PARTS, length // dirs // PARTS, 2 * length)
    both = both.transpose(2, 1, 0, 3, 4).reshape(PARTS, -1, 2 * length)
    return both.astype(ml_dtypes.bfloat16)


def inverse_table(length):
    phase = np.outer(np.arange(length), np.arange(length)) % length * (2.0 * np.pi / length)
    both = np.concatenate([np.cos(phase) / length, np.sin(phase) / length], axis=1)
    return both.astype(ml_dtypes.bfloat16)


def fused(
    dirs,
    boxes,
    source_hbm,
    offset_hbm,
    count_hbm,
    x_hbm,
    wf_hbm,
    axial_hbm,
    legendre_hbm,
    wi_hbm,
    planar_hbm,
    translator_hbm,
    out_ref,
    source_ref,
    offset_ref,
    count_ref,
    x_ref,
    wf_ref,
    axial_ref,
    legendre_ref,
    wi_ref,
    planar_ref,
    translator_ref,
    samples,
    send1,
    recv1,
    spread,
    pairs,
    send2,
    recv2,
    field,
    planar_cos,
    planar_sin,
    sums,
    stored,
    halo,
    local_sems,
    index_sems,
    send1_sems,
    recv1_sems,
    send2_sems,
    recv2_sems,
    halo_send,
    halo_recv,
):
    me = lax.axis_index("dir")
    box = lax.axis_index("box")
    right, left = lax.rem(box + 1, boxes), lax.rem(box + boxes - 1, boxes)
    rows_out, length = planar_ref.shape[1:]
    own = legendre_ref.shape[0]
    modes = own // PARTS
    rows_in = LANES // dirs
    slots = source_ref.shape[1]
    peers = (me + 1 - 2 * lax.rem(me, 2), lax.rem(me + 2, 4), 3 - me)
    inner = lax.rem((me + 1) // 2, 2)

    def peer_of(step):
        low = lax.rem(me % 2 + (step + 1) % 2, 2)
        high = lax.rem(me // 2 + (step + 1) // 2, 2)
        return low + 2 * high

    second, third = 2 * inner, 2 - 2 * inner

    barrier = pltpu.get_barrier_semaphore()
    for peer in peers:
        pl.semaphore_signal(barrier, inc=1, device_id=(box, peer), device_id_type=MESH)
    for peer in (left, right):
        pl.semaphore_signal(barrier, inc=1, device_id=(peer, me), device_id_type=MESH)

    def load(src, dst, sem):
        return pltpu.make_async_copy(src, dst, sem)

    load_x = load(x_hbm, x_ref, local_sems.at[0])
    load_wf = [load(wf_hbm.at[i], wf_ref.at[i], local_sems.at[1 + i]) for i in range(PARTS)]
    at = 1 + PARTS
    load_planar = load(planar_hbm, planar_ref, local_sems.at[at])
    load_translator = load(translator_hbm, translator_ref, local_sems.at[at + 1])
    load_legendre = load(legendre_hbm, legendre_ref, local_sems.at[at + 2])
    load_axial = load(axial_hbm, axial_ref, local_sems.at[at + 3])
    load_wi = load(wi_hbm, wi_ref, local_sems.at[at + 4])
    load_index = [
        load(src, dst, index_sems.at[i])
        for i, (src, dst) in enumerate(
            ((source_hbm, source_ref), (offset_hbm, offset_ref), (count_hbm, count_ref))
        )
    ]
    for item in (load_x, *load_wf):
        item.start()

    def out_copy(chunk, step):
        return pltpu.make_async_remote_copy(
            src_ref=send1.at[chunk, peer_of(step)],
            dst_ref=recv1.at[chunk, me],
            send_sem=send1_sems.at[chunk, step],
            recv_sem=recv1_sems.at[chunk, step],
            device_id=(box, peer_of(step)),
            device_id_type=MESH,
        )

    def back_copy(p, piece, step):
        part = slice(None) if p == 0 else piece
        index = 0 if p == 0 else 1 + piece
        return pltpu.make_async_remote_copy(
            src_ref=send2.at[p, peer_of(step), part],
            dst_ref=recv2.at[p, me, part],
            send_sem=send2_sems.at[index, step],
            recv_sem=recv2_sems.at[index, step],
            device_id=(box, peer_of(step)),
            device_id_type=MESH,
        )

    comps = LANES // rows_in
    to = lax.broadcasted_iota(jnp.int32, (LANES, LANES), 0)
    come = lax.broadcasted_iota(jnp.int32, (LANES, LANES), 1)
    sorting = ((to % rows_in) * comps + to // rows_in == come).astype(F32).astype(BF16)
    load_x.wait()
    for k in range(x_ref.shape[0]):
        sorted_rows = jnp.dot(
            sorting, x_ref[k].reshape(LANES, length), preferred_element_type=F32
        ).astype(BF16)
        for c in range(comps):
            p, r = c // 2, c % 2
            row = (p * x_ref.shape[0] + k) * rows_in
            samples[row : row + rows_in, r * length : (r + 1) * length] = sorted_rows[
                c * rows_in : (c + 1) * rows_in
            ]
    cols = samples.shape[0] // 2

    def transform(table, p):
        return lax.dot_general(
            table,
            samples[p * cols : (p + 1) * cols],
            (((1,), (1,)), ((), ())),
            preferred_element_type=F32,
        ).astype(BF16)

    for chunk in range(CHUNKS):
        p, part = chunk // PARTS, chunk % PARTS
        if p == 0:
            load_wf[part].wait()
        if chunk == 0:
            targets = (peers[1], peer_of(second), peer_of(third), me)
            for i, target in enumerate(targets):
                tall = 2 * modes
                send1[chunk, target] = transform(
                    wf_ref[part, pl.ds(pl.multiple_of(target * tall, tall), tall)], p
                )
                if i == 0:
                    pl.semaphore_wait(barrier, dirs + 1)
                if i < 2:
                    out_copy(chunk, (1, second)[i]).start()
        else:
            send1[chunk] = transform(wf_ref[part], p).reshape(send1.shape[1:])
            out_copy(chunk, 1).start()
            out_copy(chunk, second).start()
        if chunk == 0:
            for item in (load_planar, *load_index, load_translator, load_axial, load_legendre, load_wi):
                item.start()
        if part == PARTS - 1:
            for i in range(PARTS):
                out_copy(p * PARTS + i, third).start()
        recv1[chunk, me] = send1[chunk, me]

    load_planar.wait()
    for q in range(4):
        planar_cos[q] = jnp.cos(planar_ref[q])
        planar_sin[q] = jnp.sin(planar_ref[q])
    for item in load_index:
        item.wait()
    load_translator.wait()
    sums[...] = jnp.zeros_like(sums)

    def gather(slot, carry):
        source, op = source_ref[0, slot], offset_ref[0, slot]
        live = slot < count_ref[0]
        before = jnp.where(jnp.logical_and(live, source < box), 1.0, 0.0)
        after = jnp.where(jnp.logical_and(live, source > box), 1.0, 0.0)
        for r in range(2):
            tile = translator_ref[op, r].astype(F32)
            sums[0, r] += before * tile
            sums[1, r] += after * tile
        return carry

    lax.fori_loop(0, slots, gather, 0)

    load_axial.wait()
    kids = x_ref.shape[0]
    theta = axial_ref.shape[1]
    upper = lax.broadcasted_iota(jnp.int32, (kids, theta), 0) < kids // 2
    angle = jnp.where(upper, axial_ref[0:1], axial_ref[1:2])
    axial_cos, axial_sin = jnp.cos(angle), jnp.sin(angle)
    block = lax.broadcasted_iota(jnp.int32, (modes, LANES), 1) // rows_in
    lane = lax.broadcasted_iota(jnp.int32, (EXCHANGE, LANES), 1)
    load_legendre.wait()

    def exchanged(tiles, a):
        out = tiles[a]
        for s in range(4):
            if s != a:
                shift = ((s - a) * rows_in) % LANES
                out = jnp.where(block == s, pltpu.roll(tiles[s], shift, 1), out)
        return out

    def interpolate(p, part):
        chunk = p * PARTS + part
        for step in range(3):
            out_copy(chunk, step).wait_recv()
        for r in range(2):
            for g in range(kids // dirs):
                tiles = [
                    recv1[
                        chunk, s, r * modes : (r + 1) * modes, g * LANES : (g + 1) * LANES
                    ].astype(F32)
                    for s in range(dirs)
                ]
                for a in range(dirs):
                    spread[pl.ds(r * kids + g * dirs + a, modes, stride=2 * kids), :] = exchanged(
                        tiles, a
                    )
        first = part * modes

        def mode(i, inner):
            rows = spread[pl.ds(pl.multiple_of(i * 2 * kids, 2 * kids), 2 * kids), :]
            value = lax.dot_general(
                rows.astype(BF16),
                legendre_ref[first + i],
                (((1,), (1,)), ((), ())),
                preferred_element_type=F32,
            )
            real, imag = value[:kids], value[kids:]
            sum_real = real * axial_cos - imag * axial_sin
            sum_imag = real * axial_sin + imag * axial_cos
            both = jnp.where(
                upper,
                sum_real + pltpu.roll(sum_real, kids // 2, 0),
                sum_imag + pltpu.roll(sum_imag, kids // 2, 0),
            )
            for n in range(pairs.shape[0]):
                tile = pairs.at[n]
                tile[pl.ds(i, kids, stride=modes), :] = both[:, n * LANES : (n + 1) * LANES]
            return inner

        lax.fori_loop(0, modes, mode, 0, unroll=8)
        for n in range(pairs.shape[0]):
            for top in range(0, modes, EXCHANGE):
                tiles = [pairs[n, k * modes + top : k * modes + top + EXCHANGE, :] for k in range(8)]
                for bit in (1, 2, 4):
                    distance = bit * LANES // 8
                    for k in range(8):
                        if not k & bit:
                            one, two = tiles[k], tiles[k | bit]
                            clear = lane // distance % 2 == 0
                            tiles[k] = jnp.where(clear, one, pltpu.roll(two, distance, 1))
                            tiles[k | bit] = jnp.where(
                                clear, pltpu.roll(one, LANES - distance, 1), two
                            )
                rows = pl.ds(pl.multiple_of(first + top, EXCHANGE), EXCHANGE)
                for g in range(8):
                    send2[p, 2 * n + g // 4, g % 4, rows] = tiles[g].astype(BF16)

    for p in range(2):

        def both_parts(part, carry, p=p):
            interpolate(p, part)
            return carry

        lax.fori_loop(0, PARTS, both_parts, 0)
        for step in (1, second, third):
            for piece in range(1 if p == 0 else PIECES):
                back_copy(p, piece, step).start()
        recv2[p, me] = send2[p, me]

    load_wi.wait()
    has = (box < boxes - 1, box > 0)
    far = 1 - lax.rem(box, 2)

    def move(p, piece, side):
        part = slice(None) if p == 0 else piece
        index = 0 if p == 0 else 1 + piece
        return pltpu.make_async_remote_copy(
            src_ref=stored.at[p, part],
            dst_ref=halo.at[side, p, part],
            send_sem=halo_send.at[side, index],
            recv_sem=halo_recv.at[side, index],
            device_id=(box + 1 - 2 * side, me),
            device_id_type=MESH,
        )

    band = rows_out // PIECES
    for p in range(2):
        for piece in range(PIECES):
            if p == 1 or piece == 0:
                for step in range(3):
                    back_copy(p, piece, step).wait_recv()
            field[...] = lax.dot_general(
                recv2[p, :, piece].reshape(-1, LANES),
                wi_ref[...],
                (((0,), (0,)), ((), ())),
                preferred_element_type=F32,
            )
            total_real, total_imag = 0.0, 0.0
            for q in range(4):
                cos = planar_cos[q, piece * band : (piece + 1) * band]
                sin = planar_sin[q, piece * band : (piece + 1) * band]
                one = field[q * band : (q + 1) * band]
                two = field[(4 + q) * band : (5 + q) * band]
                real = one[:, :length] - two[:, length:]
                imag = one[:, length:] + two[:, :length]
                total_real = total_real + (real * cos - imag * sin)
                total_imag = total_imag + (real * sin + imag * cos)
            stored[p, piece, 0] = total_real.astype(BF16)
            stored[p, piece, 1] = total_imag.astype(BF16)
            if p == 1 or piece == PIECES - 1:
                for side in (far, 1 - far):
                    there = box + 1 - 2 * side
                    pl.when(jnp.logical_and(there >= 0, there < boxes))(move(p, piece, side).start)
    for step in range(3):
        for chunk in range(CHUNKS):
            out_copy(chunk, step).wait_send()
        for piece in range(PIECES):
            back_copy(1, piece, step).wait_send()
        back_copy(0, 0, step).wait_send()
    for p in range(2):
        for piece in range(PIECES):
            if p == 1 or piece == 0:
                for side in range(2):
                    pl.when(has[side])(move(p, piece, side).wait_send)
                    pl.when(has[1 - side])(move(p, piece, side).wait_recv)
            real, imag = 0.0, 0.0
            mine = slice(piece * band, (piece + 1) * band)
            for side in range(2):
                source_real = jnp.where(has[1 - side], halo[side, p, piece, 0].astype(F32), 0.0)
                source_imag = jnp.where(has[1 - side], halo[side, p, piece, 1].astype(F32), 0.0)
                weight_real, weight_imag = sums[side, 0, mine], sums[side, 1, mine]
                real = real + (weight_real * source_real - weight_imag * source_imag)
                imag = imag + (weight_real * source_imag + weight_imag * source_real)
            out_ref[2 * p, mine] = real.astype(BF16)
            out_ref[2 * p + 1, mine] = imag.astype(BF16)


def shards(
    children,
    legendre,
    axial_angle,
    planar_angle,
    translator,
    group_slot,
    source_list,
    offset_list,
    row_counts,
):
    local_groups, kids, rows_in, comps, length = children.shape
    dirs = lax.axis_size("dir")
    boxes = lax.axis_size("box")
    modes_local, theta_out, theta_in = legendre.shape
    rows_out = theta_out // dirs
    fits = (
        local_groups == 1
        and dirs == 4
        and boxes > 2
        and kids == 8
        and comps == 4
        and theta_in == LANES
        and 2 * rows_out == LANES
        and rows_out % (16 * PIECES) == 0
        and modes_local == LANES
    )
    if not fits:
        return general(
            children,
            legendre,
            axial_angle,
            planar_angle,
            translator,
            group_slot,
            source_list,
            offset_list,
            row_counts,
        )
    rows = kids * 2 * rows_in
    forward = jnp.asarray(forward_table(length, dirs))
    modes = modes_local // PARTS
    vmem = pl.BlockSpec(memory_space=pltpu.VMEM)
    hbm = pl.BlockSpec(memory_space=pltpu.HBM)
    inverse = jnp.asarray(inverse_table(length))
    exchange = pltpu.SemaphoreType.DMA((CHUNKS, dirs - 1))
    back = pltpu.SemaphoreType.DMA((1 + PIECES, dirs - 1))
    out = pl.pallas_call(
        functools.partial(fused, dirs, boxes),
        out_shape=jax.ShapeDtypeStruct((comps, rows_out, length), BF16),
        in_specs=[hbm] * 10,
        out_specs=vmem,
        scratch_shapes=[
            pltpu.SMEM(source_list.shape, jnp.int32),
            pltpu.SMEM(offset_list.shape, jnp.int32),
            pltpu.SMEM(row_counts.shape, jnp.int32),
            pltpu.VMEM(children.shape[1:], BF16),
            pltpu.VMEM(forward.shape, BF16),
            pltpu.VMEM(axial_angle.shape, F32),
            pltpu.VMEM(legendre.shape, BF16),
            pltpu.VMEM(inverse.shape, BF16),
            pltpu.VMEM(planar_angle.shape, F32),
            pltpu.VMEM(translator.shape, BF16),
            pltpu.VMEM((rows, 2 * length), BF16),
            pltpu.VMEM((CHUNKS, dirs, 2 * modes, rows // 2), BF16),
            pltpu.VMEM((CHUNKS, dirs, 2 * modes, rows // 2), BF16),
            pltpu.VMEM((modes * kids * 2, LANES), F32),
            pltpu.VMEM((theta_out // LANES, 8 * modes, LANES), F32),
            pltpu.VMEM((2, dirs, PIECES, modes_local, LANES), BF16),
            pltpu.VMEM((2, dirs, PIECES, modes_local, LANES), BF16),
            pltpu.VMEM((LANES, 2 * length), F32),
            pltpu.VMEM(planar_angle.shape, F32),
            pltpu.VMEM(planar_angle.shape, F32),
            pltpu.VMEM((2, 2, rows_out, length), F32),
            pltpu.VMEM((2, PIECES, 2, rows_out // PIECES, length), BF16),
            pltpu.VMEM((2, 2, PIECES, 2, rows_out // PIECES, length), BF16),
            pltpu.SemaphoreType.DMA((6 + PARTS,)),
            pltpu.SemaphoreType.DMA((3,)),
            exchange,
            exchange,
            back,
            back,
            pltpu.SemaphoreType.DMA((2, 1 + PIECES)),
            pltpu.SemaphoreType.DMA((2, 1 + PIECES)),
        ],
        compiler_params=pltpu.CompilerParams(
            collective_id=0, has_side_effects=True, vmem_limit_bytes=40 * 1024 * 1024
        ),
    )(
        pltpu.with_memory_space_constraint(source_list, pltpu.HBM),
        pltpu.with_memory_space_constraint(offset_list, pltpu.HBM),
        row_counts,
        *(
            pltpu.with_memory_space_constraint(item, pltpu.HBM)
            for item in (
                children[0],
                forward,
                axial_angle,
                legendre,
                inverse,
                planar_angle,
                translator,
            )
        ),
    )
    return out.transpose(1, 0, 2)[None]


def solution(mesh):
    placed = (
        P("box", None, "dir", None, None),
        P("dir", None, None),
        P(),
        P(None, "dir", None),
        P(None, None, "dir", None),
        P("box"),
        P("box", None),
        P("box", None),
        P("box"),
    )
    return jax.shard_map(
        shards, mesh=mesh, in_specs=placed, out_specs=P("box", "dir", None, None), check_vma=False
    )
```

```python
import functools
import math

import jax
import jax.numpy as jnp
import ml_dtypes
import numpy as np
from jax import lax
from jax.experimental import pallas as pl
from jax.experimental.pallas import tpu as pltpu
from jax.sharding import PartitionSpec as P

MESH = pl.DeviceIdType.MESH
F32 = jnp.float32
BF16 = jnp.bfloat16
LANES = 128


def extended(x, sides, width):
    for axis, dim in sides:
        peers, length = (lax.axis_size(axis), x.shape[dim])
        up = [(i, (i + 1) % peers) for i in range(peers - 1)]
        down = [(j, i) for i, j in up]
        last = lax.slice_in_dim(x, length - width, length, axis=dim)
        initial = lax.slice_in_dim(x, 0, width, axis=dim)
        before = lax.ppermute(last, axis, up)
        after = lax.ppermute(initial, axis, down)
        x = jnp.concatenate([before, x, after], axis=dim)
    return x


def dft_tables(length):
    samples = jnp.arange(length, dtype=jnp.int32)
    product = samples[:, None] * samples[None, :] % length
    phase = product.astype(jnp.float32) * (2.0 * math.pi / length)
    cosine = jnp.cos(phase) / math.sqrt(length)
    sine = jnp.sin(phase) / math.sqrt(length)
    return (cosine, sine)


def general(
    children,
    legendre,
    axial_angle,
    planar_angle,
    translator,
    group_slot,
    source_list,
    offset_list,
    row_counts,
):
    local_groups, kids, rows_in, comps, length = children.shape
    dir_count = lax.axis_size("dir")
    box_index = lax.axis_index("box")
    modes_local = legendre.shape[0]
    rows_out = legendre.shape[1] // dir_count
    cosine, sine = dft_tables(length)
    high = lax.Precision.HIGH
    values = children.astype(jnp.float32).reshape(local_groups, kids, rows_in, 2, 2, length)
    samples_real = values[..., 0, :]
    samples_imag = values[..., 1, :]
    spec_real = jnp.einsum("gkqpj,jm->mgkpq", samples_real, cosine, precision=high) + jnp.einsum(
        "gkqpj,jm->mgkpq", samples_imag, sine, precision=high
    )
    spec_imag = jnp.einsum("gkqpj,jm->mgkpq", samples_imag, cosine, precision=high) - jnp.einsum(
        "gkqpj,jm->mgkpq", samples_real, sine, precision=high
    )
    spectrum = jnp.stack([spec_real, spec_imag], axis=4)
    spectrum = spectrum.astype(jnp.bfloat16).reshape(
        1, length, local_groups * kids * comps * rows_in
    )
    received = lax.all_to_all(spectrum, "dir", split_axis=1, concat_axis=0, tiled=True)
    received = received.reshape(dir_count, modes_local, local_groups * kids * comps, rows_in)
    matrices = legendre.reshape(modes_local, dir_count, rows_out, dir_count, rows_in)
    interp = jnp.einsum("mabsq,smcq->macb", matrices, received, preferred_element_type=jnp.float32)
    interp = interp.reshape(modes_local, dir_count, local_groups, 2, 4, 2, 2, rows_out)
    angles = jnp.transpose(axial_angle.reshape(2, dir_count, rows_out), (1, 0, 2))
    axial_cos = jnp.cos(angles)[None, :, None, :, None, None, :]
    axial_sin = jnp.sin(angles)[None, :, None, :, None, None, :]
    part_real = interp[..., 0, :]
    part_imag = interp[..., 1, :]
    pairs_real = jnp.sum(part_real * axial_cos - part_imag * axial_sin, axis=3)
    pairs_imag = jnp.sum(part_real * axial_sin + part_imag * axial_cos, axis=3)
    pairs = jnp.stack([pairs_real, pairs_imag], axis=5)
    pairs = pairs.reshape(modes_local, dir_count, local_groups * 4 * 2 * 2 * rows_out)
    returned = lax.all_to_all(pairs, "dir", split_axis=1, concat_axis=0, tiled=True)
    combined = returned.reshape(length, local_groups, 4, 2, 2, rows_out)
    comb_real = combined[:, :, :, :, 0, :]
    comb_imag = combined[:, :, :, :, 1, :]
    field_real = jnp.einsum("mgxpb,mj->gxbpj", comb_real, cosine, precision=high) - jnp.einsum(
        "mgxpb,mj->gxbpj", comb_imag, sine, precision=high
    )
    field_imag = jnp.einsum("mgxpb,mj->gxbpj", comb_real, sine, precision=high) + jnp.einsum(
        "mgxpb,mj->gxbpj", comb_imag, cosine, precision=high
    )
    planar_cos = jnp.cos(planar_angle)[None, :, :, None, :]
    planar_sin = jnp.sin(planar_angle)[None, :, :, None, :]
    stored_real = jnp.sum(field_real * planar_cos - field_imag * planar_sin, axis=1)
    stored_imag = jnp.sum(field_real * planar_sin + field_imag * planar_cos, axis=1)
    stored = jnp.stack([stored_real, stored_imag], axis=3)
    stored = stored.reshape(local_groups, rows_out, comps, length).astype(jnp.bfloat16)
    local_slot = group_slot - box_index * local_groups
    placement = (local_slot[None, :] == jnp.arange(local_groups)[:, None]).astype(jnp.bfloat16)
    ordered = jnp.einsum("lk,kbcj->lbcj", placement, stored, preferred_element_type=jnp.float32)
    ordered = ordered.astype(jnp.bfloat16)
    window = extended(ordered, (("box", 0),), local_groups)
    relative = source_list - (box_index - 1) * local_groups
    near = (relative[..., None] == jnp.arange(window.shape[0])).astype(jnp.bfloat16)
    picked = jnp.einsum("glw,wbcj->glbcj", near, window, preferred_element_type=jnp.float32)
    picked = picked.reshape(local_groups, source_list.shape[1], rows_out, 2, 2, length)
    chosen = (offset_list[..., None] == jnp.arange(translator.shape[0])).astype(jnp.bfloat16)
    operator = jnp.einsum("glo,orbj->glrbj", chosen, translator, preferred_element_type=jnp.float32)
    live = (jnp.arange(source_list.shape[1])[None, :] < row_counts[:, None]).astype(jnp.float32)
    live = live[:, :, None, None, None]
    oper_real = operator[:, :, 0, :, None, :].astype(jnp.float32) * live
    oper_imag = operator[:, :, 1, :, None, :].astype(jnp.float32) * live
    picked_real = picked[..., 0, :].astype(jnp.float32)
    picked_imag = picked[..., 1, :].astype(jnp.float32)
    total_real = jnp.sum(oper_real * picked_real - oper_imag * picked_imag, axis=1)
    total_imag = jnp.sum(oper_real * picked_imag + oper_imag * picked_real, axis=1)
    result = jnp.stack([total_real, total_imag], axis=3).reshape(
        local_groups, rows_out, comps, length
    )
    return result.astype(jnp.bfloat16)


PARTS = 2
CHUNKS = 2 * PARTS
PIECES = 4
EXCHANGE = 32


def forward_table(length, dirs):
    phase = np.outer(np.arange(length), np.arange(length)) % length * (2.0 * np.pi / length)
    cosine, sine = np.cos(phase), np.sin(phase)
    both = np.stack(
        [np.concatenate([cosine, sine], axis=1), np.concatenate([-sine, cosine], axis=1)], axis=0
    )
    both = both.reshape(2, dirs, PARTS, length // dirs // PARTS, 2 * length)
    both = both.transpose(2, 1, 0, 3, 4).reshape(PARTS, -1, 2 * length)
    return both.astype(ml_dtypes.bfloat16)


def inverse_table(length):
    phase = np.outer(np.arange(length), np.arange(length)) % length * (2.0 * np.pi / length)
    both = np.concatenate([np.cos(phase) / length, np.sin(phase) / length], axis=1)
    return both.astype(ml_dtypes.bfloat16)


def fused(
    dirs,
    boxes,
    source_hbm,
    offset_hbm,
    count_hbm,
    x_hbm,
    wf_hbm,
    axial_hbm,
    legendre_hbm,
    wi_hbm,
    planar_hbm,
    translator_hbm,
    out_ref,
    source_ref,
    offset_ref,
    count_ref,
    x_ref,
    wf_ref,
    axial_ref,
    legendre_ref,
    wi_ref,
    planar_ref,
    translator_ref,
    samples,
    send1,
    recv1,
    spread,
    pairs,
    send2,
    recv2,
    field,
    planar_cos,
    planar_sin,
    sums,
    stored,
    halo,
    flat,
    local_sems,
    index_sems,
    send1_sems,
    recv1_sems,
    send2_sems,
    recv2_sems,
    halo_send,
    halo_recv,
):
    me = lax.axis_index("dir")
    box = lax.axis_index("box")
    ends = (boxes - box) // boxes + (box + 1) // boxes
    rows_out, length = planar_ref.shape[1:]
    own = legendre_ref.shape[0]
    modes = own // PARTS
    rows_in = LANES // dirs
    slots = source_ref.shape[1]
    peers = (me + 1 - 2 * lax.rem(me, 2), lax.rem(me + 2, 4), 3 - me)
    inner = lax.rem((me + 1) // 2, 2)

    def peer_of(step):
        low = lax.rem(me % 2 + (step + 1) % 2, 2)
        high = lax.rem(me // 2 + (step + 1) // 2, 2)
        return low + 2 * high

    second, third = 2 * inner, 2 - 2 * inner

    barrier = pltpu.get_barrier_semaphore()
    for peer in peers:
        pl.semaphore_signal(barrier, inc=1, device_id=(box, peer), device_id_type=MESH)
    for peer, there in ((box - 1, box > 0), (box + 1, box < boxes - 1)):

        @pl.when(there)
        def _(peer=peer):
            pl.semaphore_signal(barrier, inc=1, device_id=(peer, me), device_id_type=MESH)


    def load(src, dst, sem):
        return pltpu.make_async_copy(src, dst, sem)

    load_x = load(x_hbm, x_ref, local_sems.at[0])
    tall = wf_ref.shape[1] // dirs
    targets = (peers[1], peer_of(second), peer_of(third), me)
    bands = [pl.ds(pl.multiple_of(target * tall, tall), tall) for target in targets]
    load_first = [
        load(wf_hbm.at[0, bands[i]], wf_ref.at[0, bands[i]], local_sems.at[1 + i])
        for i in range(dirs)
    ]
    load_wf = load(wf_hbm.at[1], wf_ref.at[1], local_sems.at[1 + dirs])
    at = 2 + dirs
    load_planar = load(planar_hbm, planar_ref, local_sems.at[at])
    load_translator = load(translator_hbm, translator_ref, local_sems.at[at + 1])
    load_legendre = load(legendre_hbm, legendre_ref, local_sems.at[at + 2])
    load_axial = load(axial_hbm, axial_ref, local_sems.at[at + 3])
    load_wi = load(wi_hbm, wi_ref, local_sems.at[at + 4])
    load_index = [
        load(src, dst, index_sems.at[i])
        for i, (src, dst) in enumerate(
            ((source_hbm, source_ref), (offset_hbm, offset_ref), (count_hbm, count_ref))
        )
    ]
    for item in (load_x, *load_first, load_wf):
        item.start()

    def out_copy(chunk, step):
        return pltpu.make_async_remote_copy(
            src_ref=send1.at[chunk, peer_of(step)],
            dst_ref=recv1.at[chunk, me],
            send_sem=send1_sems.at[chunk, step],
            recv_sem=recv1_sems.at[chunk, step],
            device_id=(box, peer_of(step)),
            device_id_type=MESH,
        )

    def back_copy(p, piece, step):
        part = slice(None) if p == 0 else piece
        index = 0 if p == 0 else 1 + piece
        return pltpu.make_async_remote_copy(
            src_ref=send2.at[p, peer_of(step), part],
            dst_ref=recv2.at[p, me, part],
            send_sem=send2_sems.at[index, step],
            recv_sem=recv2_sems.at[index, step],
            device_id=(box, peer_of(step)),
            device_id_type=MESH,
        )

    comps = LANES // rows_in
    to = lax.broadcasted_iota(jnp.int32, (LANES, LANES), 0)
    come = lax.broadcasted_iota(jnp.int32, (LANES, LANES), 1)
    sorting = ((to % rows_in) * comps + to // rows_in == come).astype(F32).astype(BF16)
    load_x.wait()
    for k in range(x_ref.shape[0]):
        sorted_rows = jnp.dot(
            sorting, x_ref[k].reshape(LANES, length), preferred_element_type=F32
        ).astype(BF16)
        for c in range(comps):
            p, r = c // 2, c % 2
            row = (p * x_ref.shape[0] + k) * rows_in
            samples[row : row + rows_in, r * length : (r + 1) * length] = sorted_rows[
                c * rows_in : (c + 1) * rows_in
            ]
    cols = samples.shape[0] // 2

    def transform(table, p):
        return lax.dot_general(
            table,
            samples[p * cols : (p + 1) * cols],
            (((1,), (1,)), ((), ())),
            preferred_element_type=F32,
        ).astype(BF16)

    for chunk in range(CHUNKS):
        p, part = chunk // PARTS, chunk % PARTS
        if chunk == 1:
            load_wf.wait()
        if chunk == 0:
            for i, target in enumerate(targets):
                load_first[i].wait()
                send1[chunk, target] = transform(
                    wf_ref[part, bands[i]], p
                )
                if i == 0:
                    pl.semaphore_wait(barrier, dirs + 1 - ends)
                if i < 2:
                    out_copy(chunk, (1, second)[i]).start()
        else:
            send1[chunk] = transform(wf_ref[part], p).reshape(send1.shape[1:])
            out_copy(chunk, 1).start()
            out_copy(chunk, second).start()
        if chunk == 0:
            for item in (load_planar, *load_index, load_translator, load_axial, load_legendre, load_wi):
                item.start()
        if part == PARTS - 1:
            for i in range(PARTS):
                out_copy(p * PARTS + i, third).start()
        recv1[chunk, me] = send1[chunk, me]

    load_planar.wait()
    for q in range(4):
        planar_cos[q] = jnp.cos(planar_ref[q])
        planar_sin[q] = jnp.sin(planar_ref[q])
    for item in load_index:
        item.wait()
    load_translator.wait()
    sums[...] = jnp.zeros_like(sums)

    def gather(slot, carry):
        source, op = source_ref[0, slot], offset_ref[0, slot]
        live = slot < count_ref[0]
        before = jnp.where(jnp.logical_and(live, source < box), 1.0, 0.0)
        after = jnp.where(jnp.logical_and(live, source > box), 1.0, 0.0)
        for r in range(2):
            tile = translator_ref[op, r].astype(F32)
            sums[0, r] += before * tile
            sums[1, r] += after * tile
        return carry

    lax.fori_loop(0, slots, gather, 0)

    load_axial.wait()
    kids = x_ref.shape[0]
    theta = axial_ref.shape[1]
    upper = lax.broadcasted_iota(jnp.int32, (kids, theta), 0) < kids // 2
    angle = jnp.where(upper, axial_ref[0:1], axial_ref[1:2])
    axial_cos, axial_sin = jnp.cos(angle), jnp.sin(angle)
    block = lax.broadcasted_iota(jnp.int32, (modes, LANES), 1) // rows_in
    lane = lax.broadcasted_iota(jnp.int32, (EXCHANGE, LANES), 1)
    load_legendre.wait()

    def exchanged(tiles, a):
        out = tiles[a]
        for s in range(4):
            if s != a:
                shift = ((s - a) * rows_in) % LANES
                out = jnp.where(block == s, pltpu.roll(tiles[s], shift, 1), out)
        return out

    def interpolate(p, part):
        chunk = p * PARTS + part
        for step in range(3):
            out_copy(chunk, step).wait_recv()
        for r in range(2):
            for g in range(kids // dirs):
                tiles = [
                    recv1[
                        chunk, s, r * modes : (r + 1) * modes, g * LANES : (g + 1) * LANES
                    ].astype(F32)
                    for s in range(dirs)
                ]
                for a in range(dirs):
                    spread[pl.ds(r * kids + g * dirs + a, modes, stride=2 * kids), :] = exchanged(
                        tiles, a
                    )
        first = part * modes

        def mode(i, inner):
            rows = spread[pl.ds(pl.multiple_of(i * 2 * kids, 2 * kids), 2 * kids), :]
            value = lax.dot_general(
                rows.astype(BF16),
                legendre_ref[first + i],
                (((1,), (1,)), ((), ())),
                preferred_element_type=F32,
            )
            real, imag = value[:kids], value[kids:]
            sum_real = real * axial_cos - imag * axial_sin
            sum_imag = real * axial_sin + imag * axial_cos
            both = jnp.where(
                upper,
                sum_real + pltpu.roll(sum_real, kids // 2, 0),
                sum_imag + pltpu.roll(sum_imag, kids // 2, 0),
            )
            for n in range(pairs.shape[0]):
                tile = pairs.at[n]
                tile[pl.ds(i, kids, stride=modes), :] = both[:, n * LANES : (n + 1) * LANES]
            return inner

        lax.fori_loop(0, modes, mode, 0, unroll=8)
        for n in range(pairs.shape[0]):
            for top in range(0, modes, EXCHANGE):
                tiles = [pairs[n, k * modes + top : k * modes + top + EXCHANGE, :] for k in range(8)]
                for bit in (1, 2, 4):
                    distance = bit * LANES // 8
                    for k in range(8):
                        if not k & bit:
                            one, two = tiles[k], tiles[k | bit]
                            clear = lane // distance % 2 == 0
                            tiles[k] = jnp.where(clear, one, pltpu.roll(two, distance, 1))
                            tiles[k | bit] = jnp.where(
                                clear, pltpu.roll(one, LANES - distance, 1), two
                            )
                rows = pl.ds(pl.multiple_of(first + top, EXCHANGE), EXCHANGE)
                for g in range(8):
                    send2[p, 2 * n + g // 4, g % 4, rows] = tiles[g].astype(BF16)

    for p in range(2):

        def both_parts(part, carry, p=p):
            interpolate(p, part)
            return carry

        lax.fori_loop(0, PARTS, both_parts, 0)
        for step in (1, second, third):
            for piece in range(1 if p == 0 else PIECES):
                back_copy(p, piece, step).start()
        recv2[p, me] = send2[p, me]

    load_wi.wait()
    has = (box < boxes - 1, box > 0)
    far = 1 - lax.rem(box, 2)

    def move(p, piece, side):
        part = slice(None) if p == 0 else piece
        index = 0 if p == 0 else 1 + piece
        return pltpu.make_async_remote_copy(
            src_ref=stored.at[p, part],
            dst_ref=halo.at[side, p, part],
            send_sem=halo_send.at[side, index],
            recv_sem=halo_recv.at[side, index],
            device_id=(box + 1 - 2 * side, me),
            device_id_type=MESH,
        )

    band = rows_out // PIECES
    into = lax.broadcasted_iota(jnp.int32, (4 * band, 4 * band), 0)
    outof = lax.broadcasted_iota(jnp.int32, (4 * band, 4 * band), 1)
    final = ((into % 4) * band + into // 4 == outof).astype(F32).astype(BF16)
    for p in range(2):
        for piece in range(PIECES):
            if p == 1 or piece == 0:
                for step in range(3):
                    back_copy(p, piece, step).wait_recv()
            field[...] = lax.dot_general(
                recv2[p, :, piece].reshape(-1, LANES),
                wi_ref[...],
                (((0,), (0,)), ((), ())),
                preferred_element_type=F32,
            )
            total_real, total_imag = 0.0, 0.0
            for q in range(4):
                cos = planar_cos[q, piece * band : (piece + 1) * band]
                sin = planar_sin[q, piece * band : (piece + 1) * band]
                one = field[q * band : (q + 1) * band]
                two = field[(4 + q) * band : (5 + q) * band]
                real = one[:, :length] - two[:, length:]
                imag = one[:, length:] + two[:, :length]
                total_real = total_real + (real * cos - imag * sin)
                total_imag = total_imag + (real * sin + imag * cos)
            stored[p, piece, 0] = total_real.astype(BF16)
            stored[p, piece, 1] = total_imag.astype(BF16)
            if p == 1 or piece == PIECES - 1:
                for side in (far, 1 - far):
                    there = box + 1 - 2 * side
                    pl.when(jnp.logical_and(there >= 0, there < boxes))(move(p, piece, side).start)
    for step in range(3):
        for chunk in range(CHUNKS):
            out_copy(chunk, step).wait_send()
        for piece in range(PIECES):
            back_copy(1, piece, step).wait_send()
        back_copy(0, 0, step).wait_send()
    for p in range(2):
        for piece in range(PIECES):
            if p == 1 or piece == 0:
                for side in range(2):
                    pl.when(has[side])(move(p, piece, side).wait_send)
                    pl.when(has[1 - side])(move(p, piece, side).wait_recv)
            real, imag = 0.0, 0.0
            mine = slice(piece * band, (piece + 1) * band)
            for side in range(2):
                source_real = jnp.where(has[1 - side], halo[side, p, piece, 0].astype(F32), 0.0)
                source_imag = jnp.where(has[1 - side], halo[side, p, piece, 1].astype(F32), 0.0)
                weight_real, weight_imag = sums[side, 0, mine], sums[side, 1, mine]
                real = real + (weight_real * source_real - weight_imag * source_imag)
                imag = imag + (weight_real * source_imag + weight_imag * source_real)
            flat[piece, 2 * p * band : (2 * p + 1) * band] = real.astype(BF16)
            flat[piece, (2 * p + 1) * band : (2 * p + 2) * band] = imag.astype(BF16)
            if p == 1:
                mixed = jnp.dot(final, flat[piece], preferred_element_type=F32).astype(BF16)
                out_ref[mine] = mixed.reshape(band, 4, length)


def shards(
    children,
    legendre,
    axial_angle,
    planar_angle,
    translator,
    group_slot,
    source_list,
    offset_list,
    row_counts,
):
    local_groups, kids, rows_in, comps, length = children.shape
    dirs = lax.axis_size("dir")
    boxes = lax.axis_size("box")
    modes_local, theta_out, theta_in = legendre.shape
    rows_out = theta_out // dirs
    fits = (
        local_groups == 1
        and dirs == 4
        and boxes > 2
        and kids == 8
        and comps == 4
        and theta_in == LANES
        and 2 * rows_out == LANES
        and rows_out % (16 * PIECES) == 0
        and modes_local == LANES
    )
    if not fits:
        return general(
            children,
            legendre,
            axial_angle,
            planar_angle,
            translator,
            group_slot,
            source_list,
            offset_list,
            row_counts,
        )
    rows = kids * 2 * rows_in
    forward = jnp.asarray(forward_table(length, dirs))
    modes = modes_local // PARTS
    vmem = pl.BlockSpec(memory_space=pltpu.VMEM)
    hbm = pl.BlockSpec(memory_space=pltpu.HBM)
    inverse = jnp.asarray(inverse_table(length))
    exchange = pltpu.SemaphoreType.DMA((CHUNKS, dirs - 1))
    back = pltpu.SemaphoreType.DMA((1 + PIECES, dirs - 1))
    out = pl.pallas_call(
        functools.partial(fused, dirs, boxes),
        out_shape=jax.ShapeDtypeStruct((rows_out, comps, length), BF16),
        in_specs=[hbm] * 10,
        out_specs=vmem,
        scratch_shapes=[
            pltpu.SMEM(source_list.shape, jnp.int32),
            pltpu.SMEM(offset_list.shape, jnp.int32),
            pltpu.SMEM(row_counts.shape, jnp.int32),
            pltpu.VMEM(children.shape[1:], BF16),
            pltpu.VMEM(forward.shape, BF16),
            pltpu.VMEM(axial_angle.shape, F32),
            pltpu.VMEM(legendre.shape, BF16),
            pltpu.VMEM(inverse.shape, BF16),
            pltpu.VMEM(planar_angle.shape, F32),
            pltpu.VMEM(translator.shape, BF16),
            pltpu.VMEM((rows, 2 * length), BF16),
            pltpu.VMEM((CHUNKS, dirs, 2 * modes, rows // 2), BF16),
            pltpu.VMEM((CHUNKS, dirs, 2 * modes, rows // 2), BF16),
            pltpu.VMEM((modes * kids * 2, LANES), F32),
            pltpu.VMEM((theta_out // LANES, 8 * modes, LANES), F32),
            pltpu.VMEM((2, dirs, PIECES, modes_local, LANES), BF16),
            pltpu.VMEM((2, dirs, PIECES, modes_local, LANES), BF16),
            pltpu.VMEM((LANES, 2 * length), F32),
            pltpu.VMEM(planar_angle.shape, F32),
            pltpu.VMEM(planar_angle.shape, F32),
            pltpu.VMEM((2, 2, rows_out, length), F32),
            pltpu.VMEM((2, PIECES, 2, rows_out // PIECES, length), BF16),
            pltpu.VMEM((2, 2, PIECES, 2, rows_out // PIECES, length), BF16),
            pltpu.VMEM((PIECES, comps * rows_out // PIECES, length), BF16),
            pltpu.SemaphoreType.DMA((7 + dirs,)),
            pltpu.SemaphoreType.DMA((3,)),
            exchange,
            exchange,
            back,
            back,
            pltpu.SemaphoreType.DMA((2, 1 + PIECES)),
            pltpu.SemaphoreType.DMA((2, 1 + PIECES)),
        ],
        compiler_params=pltpu.CompilerParams(
            collective_id=0, has_side_effects=True, vmem_limit_bytes=40 * 1024 * 1024
        ),
    )(
        pltpu.with_memory_space_constraint(source_list, pltpu.HBM),
        pltpu.with_memory_space_constraint(offset_list, pltpu.HBM),
        row_counts,
        *(
            pltpu.with_memory_space_constraint(item, pltpu.HBM)
            for item in (
                children[0],
                forward,
                axial_angle,
                legendre,
                inverse,
                planar_angle,
                translator,
            )
        ),
    )
    return out[None]


def solution(mesh):
    placed = (
        P("box", None, "dir", None, None),
        P("dir", None, None),
        P(),
        P(None, "dir", None),
        P(None, None, "dir", None),
        P("box"),
        P("box", None),
        P("box", None),
        P("box"),
    )
    return jax.shard_map(
        shards, mesh=mesh, in_specs=placed, out_specs=P("box", "dir", None, None), check_vma=False
    )
```

```python
import functools
import math

import jax
import jax.numpy as jnp
import ml_dtypes
import numpy as np
from jax import lax
from jax.experimental import pallas as pl
from jax.experimental.pallas import tpu as pltpu
from jax.sharding import PartitionSpec as P

MESH = pl.DeviceIdType.MESH
F32 = jnp.float32
BF16 = jnp.bfloat16
LANES = 128


def extended(x, sides, width):
    for axis, dim in sides:
        peers, length = (lax.axis_size(axis), x.shape[dim])
        up = [(i, (i + 1) % peers) for i in range(peers - 1)]
        down = [(j, i) for i, j in up]
        last = lax.slice_in_dim(x, length - width, length, axis=dim)
        initial = lax.slice_in_dim(x, 0, width, axis=dim)
        before = lax.ppermute(last, axis, up)
        after = lax.ppermute(initial, axis, down)
        x = jnp.concatenate([before, x, after], axis=dim)
    return x


def dft_tables(length):
    samples = jnp.arange(length, dtype=jnp.int32)
    product = samples[:, None] * samples[None, :] % length
    phase = product.astype(jnp.float32) * (2.0 * math.pi / length)
    cosine = jnp.cos(phase) / math.sqrt(length)
    sine = jnp.sin(phase) / math.sqrt(length)
    return (cosine, sine)


def general(
    children,
    legendre,
    axial_angle,
    planar_angle,
    translator,
    group_slot,
    source_list,
    offset_list,
    row_counts,
):
    local_groups, kids, rows_in, comps, length = children.shape
    dir_count = lax.axis_size("dir")
    box_index = lax.axis_index("box")
    modes_local = legendre.shape[0]
    rows_out = legendre.shape[1] // dir_count
    cosine, sine = dft_tables(length)
    high = lax.Precision.HIGH
    values = children.astype(jnp.float32).reshape(local_groups, kids, rows_in, 2, 2, length)
    samples_real = values[..., 0, :]
    samples_imag = values[..., 1, :]
    spec_real = jnp.einsum("gkqpj,jm->mgkpq", samples_real, cosine, precision=high) + jnp.einsum(
        "gkqpj,jm->mgkpq", samples_imag, sine, precision=high
    )
    spec_imag = jnp.einsum("gkqpj,jm->mgkpq", samples_imag, cosine, precision=high) - jnp.einsum(
        "gkqpj,jm->mgkpq", samples_real, sine, precision=high
    )
    spectrum = jnp.stack([spec_real, spec_imag], axis=4)
    spectrum = spectrum.astype(jnp.bfloat16).reshape(
        1, length, local_groups * kids * comps * rows_in
    )
    received = lax.all_to_all(spectrum, "dir", split_axis=1, concat_axis=0, tiled=True)
    received = received.reshape(dir_count, modes_local, local_groups * kids * comps, rows_in)
    matrices = legendre.reshape(modes_local, dir_count, rows_out, dir_count, rows_in)
    interp = jnp.einsum("mabsq,smcq->macb", matrices, received, preferred_element_type=jnp.float32)
    interp = interp.reshape(modes_local, dir_count, local_groups, 2, 4, 2, 2, rows_out)
    angles = jnp.transpose(axial_angle.reshape(2, dir_count, rows_out), (1, 0, 2))
    axial_cos = jnp.cos(angles)[None, :, None, :, None, None, :]
    axial_sin = jnp.sin(angles)[None, :, None, :, None, None, :]
    part_real = interp[..., 0, :]
    part_imag = interp[..., 1, :]
    pairs_real = jnp.sum(part_real * axial_cos - part_imag * axial_sin, axis=3)
    pairs_imag = jnp.sum(part_real * axial_sin + part_imag * axial_cos, axis=3)
    pairs = jnp.stack([pairs_real, pairs_imag], axis=5)
    pairs = pairs.reshape(modes_local, dir_count, local_groups * 4 * 2 * 2 * rows_out)
    returned = lax.all_to_all(pairs, "dir", split_axis=1, concat_axis=0, tiled=True)
    combined = returned.reshape(length, local_groups, 4, 2, 2, rows_out)
    comb_real = combined[:, :, :, :, 0, :]
    comb_imag = combined[:, :, :, :, 1, :]
    field_real = jnp.einsum("mgxpb,mj->gxbpj", comb_real, cosine, precision=high) - jnp.einsum(
        "mgxpb,mj->gxbpj", comb_imag, sine, precision=high
    )
    field_imag = jnp.einsum("mgxpb,mj->gxbpj", comb_real, sine, precision=high) + jnp.einsum(
        "mgxpb,mj->gxbpj", comb_imag, cosine, precision=high
    )
    planar_cos = jnp.cos(planar_angle)[None, :, :, None, :]
    planar_sin = jnp.sin(planar_angle)[None, :, :, None, :]
    stored_real = jnp.sum(field_real * planar_cos - field_imag * planar_sin, axis=1)
    stored_imag = jnp.sum(field_real * planar_sin + field_imag * planar_cos, axis=1)
    stored = jnp.stack([stored_real, stored_imag], axis=3)
    stored = stored.reshape(local_groups, rows_out, comps, length).astype(jnp.bfloat16)
    local_slot = group_slot - box_index * local_groups
    placement = (local_slot[None, :] == jnp.arange(local_groups)[:, None]).astype(jnp.bfloat16)
    ordered = jnp.einsum("lk,kbcj->lbcj", placement, stored, preferred_element_type=jnp.float32)
    ordered = ordered.astype(jnp.bfloat16)
    window = extended(ordered, (("box", 0),), local_groups)
    relative = source_list - (box_index - 1) * local_groups
    near = (relative[..., None] == jnp.arange(window.shape[0])).astype(jnp.bfloat16)
    picked = jnp.einsum("glw,wbcj->glbcj", near, window, preferred_element_type=jnp.float32)
    picked = picked.reshape(local_groups, source_list.shape[1], rows_out, 2, 2, length)
    chosen = (offset_list[..., None] == jnp.arange(translator.shape[0])).astype(jnp.bfloat16)
    operator = jnp.einsum("glo,orbj->glrbj", chosen, translator, preferred_element_type=jnp.float32)
    live = (jnp.arange(source_list.shape[1])[None, :] < row_counts[:, None]).astype(jnp.float32)
    live = live[:, :, None, None, None]
    oper_real = operator[:, :, 0, :, None, :].astype(jnp.float32) * live
    oper_imag = operator[:, :, 1, :, None, :].astype(jnp.float32) * live
    picked_real = picked[..., 0, :].astype(jnp.float32)
    picked_imag = picked[..., 1, :].astype(jnp.float32)
    total_real = jnp.sum(oper_real * picked_real - oper_imag * picked_imag, axis=1)
    total_imag = jnp.sum(oper_real * picked_imag + oper_imag * picked_real, axis=1)
    result = jnp.stack([total_real, total_imag], axis=3).reshape(
        local_groups, rows_out, comps, length
    )
    return result.astype(jnp.bfloat16)


PARTS = 2
CHUNKS = 2 * PARTS
PIECES = 4
EXCHANGE = 32


def forward_table(length, dirs):
    phase = np.outer(np.arange(length), np.arange(length)) % length * (2.0 * np.pi / length)
    cosine, sine = np.cos(phase), np.sin(phase)
    both = np.stack(
        [np.concatenate([cosine, sine], axis=1), np.concatenate([-sine, cosine], axis=1)], axis=0
    )
    both = both.reshape(2, dirs, PARTS, length // dirs // PARTS, 2 * length)
    both = both.transpose(2, 1, 0, 3, 4).reshape(PARTS, -1, 2 * length)
    return both.astype(ml_dtypes.bfloat16)


def inverse_table(length):
    phase = np.outer(np.arange(length), np.arange(length)) % length * (2.0 * np.pi / length)
    both = np.concatenate([np.cos(phase) / length, np.sin(phase) / length], axis=1)
    return both.astype(ml_dtypes.bfloat16)


def fused(
    dirs,
    boxes,
    source_hbm,
    offset_hbm,
    count_hbm,
    x_hbm,
    wf_hbm,
    axial_hbm,
    legendre_hbm,
    wi_hbm,
    planar_hbm,
    translator_hbm,
    out_ref,
    source_ref,
    offset_ref,
    count_ref,
    x_ref,
    wf_ref,
    axial_ref,
    legendre_ref,
    wi_ref,
    planar_ref,
    translator_ref,
    samples,
    send1,
    recv1,
    spread,
    pairs,
    send2,
    recv2,
    field,
    planar_cos,
    planar_sin,
    sums,
    stored,
    halo,
    flat,
    local_sems,
    index_sems,
    send1_sems,
    recv1_sems,
    send2_sems,
    recv2_sems,
    halo_send,
    halo_recv,
):
    me = lax.axis_index("dir")
    box = lax.axis_index("box")
    ends = (boxes - box) // boxes + (box + 1) // boxes
    rows_out, length = planar_ref.shape[1:]
    own = legendre_ref.shape[0]
    modes = own // PARTS
    rows_in = LANES // dirs
    slots = source_ref.shape[1]
    peers = (me + 1 - 2 * lax.rem(me, 2), lax.rem(me + 2, 4), 3 - me)
    inner = lax.rem((me + 1) // 2, 2)

    def peer_of(step):
        low = lax.rem(me % 2 + (step + 1) % 2, 2)
        high = lax.rem(me // 2 + (step + 1) // 2, 2)
        return low + 2 * high

    second, third = 2 * inner, 2 - 2 * inner

    barrier = pltpu.get_barrier_semaphore()
    for peer in peers:
        pl.semaphore_signal(barrier, inc=1, device_id=(box, peer), device_id_type=MESH)
    for peer, there in ((box - 1, box > 0), (box + 1, box < boxes - 1)):

        @pl.when(there)
        def _(peer=peer):
            pl.semaphore_signal(barrier, inc=1, device_id=(peer, me), device_id_type=MESH)


    def load(src, dst, sem):
        return pltpu.make_async_copy(src, dst, sem)

    load_x = load(x_hbm, x_ref, local_sems.at[0])
    tall = wf_ref.shape[1] // dirs
    targets = (peers[1], peer_of(second), peer_of(third), me)
    bands = [pl.ds(pl.multiple_of(target * tall, tall), tall) for target in targets]
    load_first = [
        load(wf_hbm.at[0, bands[i]], wf_ref.at[0, bands[i]], local_sems.at[1 + i])
        for i in range(dirs)
    ]
    load_wf = load(wf_hbm.at[1], wf_ref.at[1], local_sems.at[1 + dirs])
    at = 2 + dirs
    load_planar = load(planar_hbm, planar_ref, local_sems.at[at])
    load_translator = load(translator_hbm, translator_ref, local_sems.at[at + 1])
    load_legendre = load(legendre_hbm, legendre_ref, local_sems.at[at + 2])
    load_axial = load(axial_hbm, axial_ref, local_sems.at[at + 3])
    load_wi = load(wi_hbm, wi_ref, local_sems.at[at + 4])
    load_index = [
        load(src, dst, index_sems.at[i])
        for i, (src, dst) in enumerate(
            ((source_hbm, source_ref), (offset_hbm, offset_ref), (count_hbm, count_ref))
        )
    ]
    for item in (load_x, *load_first, load_wf):
        item.start()

    def out_copy(chunk, step):
        return pltpu.make_async_remote_copy(
            src_ref=send1.at[chunk, peer_of(step)],
            dst_ref=recv1.at[chunk, me],
            send_sem=send1_sems.at[chunk, step],
            recv_sem=recv1_sems.at[chunk, step],
            device_id=(box, peer_of(step)),
            device_id_type=MESH,
        )

    def back_copy(p, piece, step):
        part = slice(None) if p == 0 else piece
        index = 0 if p == 0 else 1 + piece
        return pltpu.make_async_remote_copy(
            src_ref=send2.at[p, peer_of(step), part],
            dst_ref=recv2.at[p, me, part],
            send_sem=send2_sems.at[index, step],
            recv_sem=recv2_sems.at[index, step],
            device_id=(box, peer_of(step)),
            device_id_type=MESH,
        )

    comps = LANES // rows_in
    to = lax.broadcasted_iota(jnp.int32, (LANES, LANES), 0)
    come = lax.broadcasted_iota(jnp.int32, (LANES, LANES), 1)
    sorting = ((to % rows_in) * comps + to // rows_in == come).astype(F32).astype(BF16)
    load_x.wait()
    for k in range(x_ref.shape[0]):
        sorted_rows = jnp.dot(
            sorting, x_ref[k].reshape(LANES, length), preferred_element_type=F32
        ).astype(BF16)
        for c in range(comps):
            p, r = c // 2, c % 2
            row = (p * x_ref.shape[0] + k) * rows_in
            samples[row : row + rows_in, r * length : (r + 1) * length] = sorted_rows[
                c * rows_in : (c + 1) * rows_in
            ]
    cols = samples.shape[0] // 2

    def transform(table, p):
        return lax.dot_general(
            table,
            samples[p * cols : (p + 1) * cols],
            (((1,), (1,)), ((), ())),
            preferred_element_type=F32,
        ).astype(BF16)

    for chunk in range(CHUNKS):
        p, part = chunk // PARTS, chunk % PARTS
        if chunk == 1:
            load_wf.wait()
        if chunk == 0:
            for i, target in enumerate(targets):
                load_first[i].wait()
                send1[chunk, target] = transform(
                    wf_ref[part, bands[i]], p
                )
                if i == 0:
                    pl.semaphore_wait(barrier, dirs + 1 - ends)
                if i < 2:
                    out_copy(chunk, (1, second)[i]).start()
        else:
            send1[chunk] = transform(wf_ref[part], p).reshape(send1.shape[1:])
            out_copy(chunk, 1).start()
            out_copy(chunk, second).start()
        if chunk == 0:
            for item in (load_planar, *load_index, load_translator, load_axial, load_legendre, load_wi):
                item.start()
        if part == PARTS - 1:
            for i in range(PARTS):
                out_copy(p * PARTS + i, third).start()
        recv1[chunk, me] = send1[chunk, me]

    load_planar.wait()
    for q in range(4):
        planar_cos[q] = jnp.cos(planar_ref[q])
        planar_sin[q] = jnp.sin(planar_ref[q])
    for item in load_index:
        item.wait()
    load_translator.wait()
    sums[...] = jnp.zeros_like(sums)

    def gather(slot, carry):
        source, op = source_ref[0, slot], offset_ref[0, slot]
        live = slot < count_ref[0]
        before = jnp.where(jnp.logical_and(live, source < box), 1.0, 0.0)
        after = jnp.where(jnp.logical_and(live, source > box), 1.0, 0.0)
        for r in range(2):
            tile = translator_ref[op, r].astype(F32)
            sums[0, r] += before * tile
            sums[1, r] += after * tile
        return carry

    lax.fori_loop(0, slots, gather, 0)

    load_axial.wait()
    kids = x_ref.shape[0]
    theta = axial_ref.shape[1]
    upper = lax.broadcasted_iota(jnp.int32, (kids, theta), 0) < kids // 2
    angle = jnp.where(upper, axial_ref[0:1], axial_ref[1:2])
    axial_cos, axial_sin = jnp.cos(angle), jnp.sin(angle)
    block = lax.broadcasted_iota(jnp.int32, (modes, LANES), 1) // rows_in
    lane = lax.broadcasted_iota(jnp.int32, (EXCHANGE, LANES), 1)
    load_legendre.wait()

    def exchanged(tiles, a):
        out = tiles[a]
        for s in range(4):
            if s != a:
                shift = ((s - a) * rows_in) % LANES
                out = jnp.where(block == s, pltpu.roll(tiles[s], shift, 1), out)
        return out

    def interpolate(p, part):
        chunk = p * PARTS + part
        for step in range(3):
            out_copy(chunk, step).wait_recv()
        for r in range(2):
            for g in range(kids // dirs):
                tiles = [
                    recv1[
                        chunk, s, r * modes : (r + 1) * modes, g * LANES : (g + 1) * LANES
                    ].astype(F32)
                    for s in range(dirs)
                ]
                for a in range(dirs):
                    spread[pl.ds(r * kids + g * dirs + a, modes, stride=2 * kids), :] = exchanged(
                        tiles, a
                    )
        first = part * modes

        def mode(i, inner):
            rows = spread[pl.ds(pl.multiple_of(i * 2 * kids, 2 * kids), 2 * kids), :]
            value = lax.dot_general(
                rows.astype(BF16),
                legendre_ref[first + i],
                (((1,), (1,)), ((), ())),
                preferred_element_type=F32,
            )
            real, imag = value[:kids], value[kids:]
            sum_real = real * axial_cos - imag * axial_sin
            sum_imag = real * axial_sin + imag * axial_cos
            both = jnp.where(
                upper,
                sum_real + pltpu.roll(sum_real, kids // 2, 0),
                sum_imag + pltpu.roll(sum_imag, kids // 2, 0),
            )
            for n in range(pairs.shape[0]):
                tile = pairs.at[n]
                tile[pl.ds(i, kids, stride=modes), :] = both[:, n * LANES : (n + 1) * LANES]
            return inner

        lax.fori_loop(0, modes, mode, 0, unroll=8)
        for n in range(pairs.shape[0]):
            for top in range(0, modes, EXCHANGE):
                tiles = [pairs[n, k * modes + top : k * modes + top + EXCHANGE, :] for k in range(8)]
                for bit in (1, 2, 4):
                    distance = bit * LANES // 8
                    for k in range(8):
                        if not k & bit:
                            one, two = tiles[k], tiles[k | bit]
                            clear = lane // distance % 2 == 0
                            tiles[k] = jnp.where(clear, one, pltpu.roll(two, distance, 1))
                            tiles[k | bit] = jnp.where(
                                clear, pltpu.roll(one, LANES - distance, 1), two
                            )
                rows = pl.ds(pl.multiple_of(first + top, EXCHANGE), EXCHANGE)
                for g in range(8):
                    send2[p, 2 * n + g // 4, g % 4, rows] = tiles[g].astype(BF16)

    for p in range(2):

        def both_parts(part, carry, p=p):
            interpolate(p, part)
            return carry

        lax.fori_loop(0, PARTS, both_parts, 0)
        for step in (1, second, third):
            for piece in range(1 if p == 0 else PIECES):
                back_copy(p, piece, step).start()
        recv2[p, me] = send2[p, me]

    load_wi.wait()
    has = (box < boxes - 1, box > 0)
    far = 1 - lax.rem(box, 2)

    def move(p, piece, side):
        part = slice(None) if p == 0 else piece
        index = 0 if p == 0 else 1 + piece
        return pltpu.make_async_remote_copy(
            src_ref=stored.at[p, part],
            dst_ref=halo.at[side, p, part],
            send_sem=halo_send.at[side, index],
            recv_sem=halo_recv.at[side, index],
            device_id=(box + 1 - 2 * side, me),
            device_id_type=MESH,
        )

    band = rows_out // PIECES
    into = lax.broadcasted_iota(jnp.int32, (4 * band, 4 * band), 0)
    outof = lax.broadcasted_iota(jnp.int32, (4 * band, 4 * band), 1)
    final = ((into % 4) * band + into // 4 == outof).astype(F32).astype(BF16)
    for p in range(2):
        for piece in range(PIECES):
            if p == 1 or piece == 0:
                for step in range(3):
                    back_copy(p, piece, step).wait_recv()
            field[...] = lax.dot_general(
                recv2[p, :, piece].reshape(-1, LANES),
                wi_ref[...],
                (((0,), (0,)), ((), ())),
                preferred_element_type=F32,
            )
            total_real, total_imag = 0.0, 0.0
            for q in range(4):
                cos = planar_cos[q, piece * band : (piece + 1) * band]
                sin = planar_sin[q, piece * band : (piece + 1) * band]
                one = field[q * band : (q + 1) * band]
                two = field[(4 + q) * band : (5 + q) * band]
                real = one[:, :length] - two[:, length:]
                imag = one[:, length:] + two[:, :length]
                total_real = total_real + (real * cos - imag * sin)
                total_imag = total_imag + (real * sin + imag * cos)
            stored[p, piece, 0] = total_real.astype(BF16)
            stored[p, piece, 1] = total_imag.astype(BF16)
            if p == 1 or piece == PIECES - 1:
                there = box + 1 - 2 * far
                pl.when(jnp.logical_and(there >= 0, there < boxes))(move(p, piece, far).start)
                if piece == PIECES - 1:
                    for item in range(PIECES if p else 1):
                        move(p, item, 1 - far).start()
    for step in range(3):
        for chunk in range(CHUNKS):
            out_copy(chunk, step).wait_send()
        for piece in range(PIECES):
            back_copy(1, piece, step).wait_send()
        back_copy(0, 0, step).wait_send()
    for p in range(2):
        for piece in range(PIECES):
            if p == 1 or piece == 0:
                for side in range(2):
                    pl.when(has[side])(move(p, piece, side).wait_send)
                    pl.when(has[1 - side])(move(p, piece, side).wait_recv)
            real, imag = 0.0, 0.0
            mine = slice(piece * band, (piece + 1) * band)
            for side in range(2):
                source_real = jnp.where(has[1 - side], halo[side, p, piece, 0].astype(F32), 0.0)
                source_imag = jnp.where(has[1 - side], halo[side, p, piece, 1].astype(F32), 0.0)
                weight_real, weight_imag = sums[side, 0, mine], sums[side, 1, mine]
                real = real + (weight_real * source_real - weight_imag * source_imag)
                imag = imag + (weight_real * source_imag + weight_imag * source_real)
            flat[piece, 2 * p * band : (2 * p + 1) * band] = real.astype(BF16)
            flat[piece, (2 * p + 1) * band : (2 * p + 2) * band] = imag.astype(BF16)
            if p == 1:
                mixed = jnp.dot(final, flat[piece], preferred_element_type=F32).astype(BF16)
                out_ref[mine] = mixed.reshape(band, 4, length)


def shards(
    children,
    legendre,
    axial_angle,
    planar_angle,
    translator,
    group_slot,
    source_list,
    offset_list,
    row_counts,
):
    local_groups, kids, rows_in, comps, length = children.shape
    dirs = lax.axis_size("dir")
    boxes = lax.axis_size("box")
    modes_local, theta_out, theta_in = legendre.shape
    rows_out = theta_out // dirs
    fits = (
        local_groups == 1
        and dirs == 4
        and boxes > 2
        and kids == 8
        and comps == 4
        and theta_in == LANES
        and 2 * rows_out == LANES
        and rows_out % (16 * PIECES) == 0
        and modes_local == LANES
    )
    if not fits:
        return general(
            children,
            legendre,
            axial_angle,
            planar_angle,
            translator,
            group_slot,
            source_list,
            offset_list,
            row_counts,
        )
    rows = kids * 2 * rows_in
    forward = jnp.asarray(forward_table(length, dirs))
    modes = modes_local // PARTS
    vmem = pl.BlockSpec(memory_space=pltpu.VMEM)
    hbm = pl.BlockSpec(memory_space=pltpu.HBM)
    inverse = jnp.asarray(inverse_table(length))
    exchange = pltpu.SemaphoreType.DMA((CHUNKS, dirs - 1))
    back = pltpu.SemaphoreType.DMA((1 + PIECES, dirs - 1))
    out = pl.pallas_call(
        functools.partial(fused, dirs, boxes),
        out_shape=jax.ShapeDtypeStruct((rows_out, comps, length), BF16),
        in_specs=[hbm] * 10,
        out_specs=vmem,
        scratch_shapes=[
            pltpu.SMEM(source_list.shape, jnp.int32),
            pltpu.SMEM(offset_list.shape, jnp.int32),
            pltpu.SMEM(row_counts.shape, jnp.int32),
            pltpu.VMEM(children.shape[1:], BF16),
            pltpu.VMEM(forward.shape, BF16),
            pltpu.VMEM(axial_angle.shape, F32),
            pltpu.VMEM(legendre.shape, BF16),
            pltpu.VMEM(inverse.shape, BF16),
            pltpu.VMEM(planar_angle.shape, F32),
            pltpu.VMEM(translator.shape, BF16),
            pltpu.VMEM((rows, 2 * length), BF16),
            pltpu.VMEM((CHUNKS, dirs, 2 * modes, rows // 2), BF16),
            pltpu.VMEM((CHUNKS, dirs, 2 * modes, rows // 2), BF16),
            pltpu.VMEM((modes * kids * 2, LANES), F32),
            pltpu.VMEM((theta_out // LANES, 8 * modes, LANES), F32),
            pltpu.VMEM((2, dirs, PIECES, modes_local, LANES), BF16),
            pltpu.VMEM((2, dirs, PIECES, modes_local, LANES), BF16),
            pltpu.VMEM((LANES, 2 * length), F32),
            pltpu.VMEM(planar_angle.shape, F32),
            pltpu.VMEM(planar_angle.shape, F32),
            pltpu.VMEM((2, 2, rows_out, length), F32),
            pltpu.VMEM((2, PIECES, 2, rows_out // PIECES, length), BF16),
            pltpu.VMEM((2, 2, PIECES, 2, rows_out // PIECES, length), BF16),
            pltpu.VMEM((PIECES, comps * rows_out // PIECES, length), BF16),
            pltpu.SemaphoreType.DMA((7 + dirs,)),
            pltpu.SemaphoreType.DMA((3,)),
            exchange,
            exchange,
            back,
            back,
            pltpu.SemaphoreType.DMA((2, 1 + PIECES)),
            pltpu.SemaphoreType.DMA((2, 1 + PIECES)),
        ],
        compiler_params=pltpu.CompilerParams(
            collective_id=0, has_side_effects=True, vmem_limit_bytes=40 * 1024 * 1024
        ),
    )(
        pltpu.with_memory_space_constraint(source_list, pltpu.HBM),
        pltpu.with_memory_space_constraint(offset_list, pltpu.HBM),
        row_counts,
        *(
            pltpu.with_memory_space_constraint(item, pltpu.HBM)
            for item in (
                children[0],
                forward,
                axial_angle,
                legendre,
                inverse,
                planar_angle,
                translator,
            )
        ),
    )
    return out[None]


def solution(mesh):
    placed = (
        P("box", None, "dir", None, None),
        P("dir", None, None),
        P(),
        P(None, "dir", None),
        P(None, None, "dir", None),
        P("box"),
        P("box", None),
        P("box", None),
        P("box"),
    )
    return jax.shard_map(
        shards, mesh=mesh, in_specs=placed, out_specs=P("box", "dir", None, None), check_vma=False
    )
```
